128 devices in a mesh: row: 4 (over x), col: 2 (over core), depth: 16 (over z, y).
Axes of the slice: x: 4, y: 4, z: 4, core: 2. Of those that a mesh axis runs over, the one named last changes fastest.
Arguments:
- grad_out: bfloat16 [16, 512, 4096], P('depth', 'row', 'col'), may hold values from -6 to 6
- gate_pre: bfloat16 [16, 512, 14336], P('depth', 'col', 'row'), may hold values from -8 to 8
- up_pre: bfloat16 [16, 512, 14336], P('depth', 'col', 'row'), may hold values from -6 to 6
- down_weight: bfloat16 [14336, 4096], P('row', 'col'), may hold values from -0.09375 to 0.09375
Outputs:
- grad_gate: bfloat16 [16, 512, 14336], P('depth', 'col', 'row')
- grad_up: bfloat16 [16, 512, 14336], P('depth', 'col', 'row')
- grad_weight: bfloat16 [14336, 4096], P('row', ('col', 'depth'))
The draws below stay inside these ranges and needn't reach their ends.
All inputs are finite; a program needn't handle non-finite values.
Results may differ from the reference program's by a relative error of at most 0.019.
Values may be sent and summed in bfloat16 or wider, within the bound.
A program may use at most 128 MiB of HBM per device.

```python
import jax
import jax.numpy as jnp
from jax import lax

D = 4096
FF = 14336
GROUPS = 16
GROUP_TOKENS = 512
TOKENS = 8192
N_COL = 2


def spiked(values, key, source, target, shards_of, factor):
    def block_of(position):
        return (jnp.arange(values.shape[position]) // (values.shape[position] // shards_of)).reshape((-1,) + (1,) * (values.ndim - 1 - position))

    near = jax.random.permutation(key, shards_of)[block_of(target)]
    other_side = (block_of(target) + shards_of // 2) % shards_of
    return jnp.where((block_of(source) == near) | (block_of(source) == other_side), factor * values, values)


def level_of(stream_key, shape, split, low, high):
    gain, own = 1.0, jax.random.fold_in(stream_key, 6)
    for dim, blocks in split:
        draws = jnp.exp(jax.random.uniform(jax.random.fold_in(own, dim), (blocks,), jnp.float32, low / len(split), high / len(split)))
        gain = gain * jnp.repeat(draws, shape[dim] // blocks).reshape([-1 if axis == dim else 1 for axis in range(len(shape))])
    return gain


def gaussian(key, shape, width, reach, cuts=(), kind=jnp.bfloat16):
    result = jax.random.normal(key, shape, jnp.float32) * width
    if len(cuts) > 0:
        result = level_of(key, shape, cuts, -0.22, 0.18) * result
    return jnp.clip(result, min=-reach, max=reach).astype(kind)


def gaussian_with(own_key, dims, scale, reach, shards, heavy, dtype=jnp.bfloat16):
    result = scale * jax.random.normal(own_key, dims, jnp.float32)
    if shards:
        result = result * level_of(own_key, dims, shards, -0.22, 0.18)
    return jnp.clip(spiked(result, jax.random.fold_in(own_key, 3), *heavy), -reach, reach).astype(dtype)


def setup_inputs(seed: int = 0) -> dict:
    keys = jax.random.split(jax.random.key(seed), 5)
    grad_out = gaussian_with(keys[0], (GROUPS, GROUP_TOKENS, D), 1.0, 6.0, ((0, 16), (1, 4), (2, 2)), (0, 2, 16, 2.0))
    gate_pre = gaussian(keys[1], (GROUPS, GROUP_TOKENS, FF), 1.5, 8.0, ((0, 16), (1, 2), (2, 4)))
    up_pre = gaussian(keys[2], (GROUPS, GROUP_TOKENS, FF), 1.0, 6.0, ((0, 16), (1, 2), (2, 4)))
    down_weight = gaussian(keys[3], (FF, D), D ** -0.5, 0.09375, ((0, 4), (1, 2)))
    return {"grad_out": grad_out, "gate_pre": gate_pre, "up_pre": up_pre, "down_weight": down_weight}


def reference(grad_out, gate_pre, up_pre, down_weight):
    gate_value = gate_pre.astype(jnp.float32)
    up_value = up_pre.astype(jnp.float32)
    sigmoid_gate = jax.nn.sigmoid(gate_value)
    silu_gate = gate_value * sigmoid_gate
    hidden = (silu_gate * up_value).astype(jnp.bfloat16)
    flat_grad = grad_out.reshape(TOKENS, D)
    block_width = D // N_COL
    grad_hidden = jnp.zeros((TOKENS, FF), jnp.float32)
    for column_index in range(N_COL):
        lower = column_index * block_width
        partial_sum = lax.dot_general(flat_grad[:, lower:lower + block_width], down_weight[:, lower:lower + block_width], (((1,), (1,)), ((), ())), preferred_element_type=jnp.float32)
        rounded = lax.optimization_barrier(partial_sum.astype(jnp.bfloat16))
        grad_hidden = grad_hidden + rounded.astype(jnp.float32)
    grad_hidden = grad_hidden.reshape(GROUPS, GROUP_TOKENS, FF)
    derivative = sigmoid_gate * (1.0 + gate_value * (1.0 - sigmoid_gate))
    grad_gate = (grad_hidden * up_value * derivative).astype(jnp.bfloat16)
    grad_up = (grad_hidden * silu_gate).astype(jnp.bfloat16)
    weight_sum = jnp.zeros((FF, D), jnp.float32)
    for group_index in range(GROUPS):
        partial_weight = lax.dot_general(hidden[group_index], grad_out[group_index], (((0,), (0,)), ((), ())), preferred_element_type=jnp.float32)
        rounded_weight = lax.optimization_barrier(partial_weight.astype(jnp.bfloat16))
        weight_sum = weight_sum + rounded_weight.astype(jnp.float32)
    token_scale = float(TOKENS) ** -0.5
    grad_weight = (weight_sum * token_scale).astype(jnp.bfloat16)
    return grad_gate, grad_up, grad_weight
```

```python
import jax
import jax.numpy as jnp
from jax import lax
from jax.experimental import pallas as pl
from jax.experimental.pallas import tpu as pltpu
from jax.sharding import PartitionSpec as P

MESH = pl.DeviceIdType.MESH
BF16, F32 = jnp.bfloat16, jnp.float32

TOK, FF, DM = 512, 3584, 2048
HALF = TOK // 2
ROWS = TOK // 4
FC = 512
HF = FC // 2
NC = FF // FC
BLK = 128
STEP = 32
SCALE = float(16 * TOK) ** -0.5


def kernel(
    go, gate, up, w, o_gate, o_up, o_w,
    g_own, g_pair, g_t, hid, gate_v, up_v, wbuf, ghs, ghr, wout,
    zs0, zr0, zs1, zr1, es, er, zkeep,
    as_, ar, ys0, yr0, ys1, yr1, ykeep,
    xo_s, xo_r, xf_s, xf_r, pp_s, pp_r, px_s, px_r, pf_s, pf_r,
    hc_s, hc_r, hp_s, hp_r, hf_s, hf_r,
    z0_s, z0_r, z1_s, z1_r, e_s, e_r, a_s, a_r, y0_s, y0_r, y1_s, y1_r,
    gh_s, gh_r, ld_g, ld_u, ld_o, ld_w, st_g, st_u, st_w,
):
    x, c, q = lax.axis_index("row"), lax.axis_index("col"), lax.axis_index("depth")
    z, y = lax.div(q, 4), lax.rem(q, 4)
    odd = lax.rem(y, 2)
    y_pair = y + 1 - 2 * odd
    y_sum = lax.rem(y + 3 + 2 * odd, 4)
    y_pair_sum = lax.rem(y_pair + 3 + 2 * (1 - odd), 4)
    core = (x, 1 - c, q)
    right, left = (lax.rem(x + 1, 4), c, q), (lax.rem(x + 3, 4), c, q)
    sides = (right, left)
    pair = (x, c, z * 4 + y_pair)
    across = (x, c, z * 4 + y_sum)
    above, below = (x, c, lax.rem(z + 1, 4) * 4 + y), (x, c, lax.rem(z + 3, 4) * 4 + y)

    barrier = pltpu.get_barrier_semaphore()
    for other in (core, right, left, pair, across, above, below):
        pl.semaphore_signal(barrier, inc=1, device_id=other, device_id_type=MESH)
    pl.semaphore_wait(barrier, 7)

    def send(src, dst, ss, rs, device):
        return pltpu.make_async_remote_copy(
            src_ref=src, dst_ref=dst, send_sem=ss, recv_sem=rs, device_id=device, device_id_type=MESH
        )

    def ds(start, size, unit):
        return pl.ds(pl.multiple_of(start, unit), size)

    def layer(j):
        return lax.rem(z + jnp.where(j == 0, 2, jnp.where(j == 1, 1, jnp.where(j == 2, 3, 0))), 4)

    def block_of(j, s):
        column = (y, y_sum, y_pair, y_pair_sum)[s]
        return layer(j) * 4 + column

    def cols(b):
        return ds(b * BLK, BLK, BLK)

    def own_copy():
        return pltpu.make_async_copy(go, g_own.at[ds(x * ROWS, ROWS, ROWS)], ld_o)

    def own_direct(b, side):
        return send(
            go.at[:, cols(b)], g_own.at[ds(x * ROWS, ROWS, ROWS), cols(b)],
            xo_s.at[b, side], xo_r.at[b, side], sides[side],
        )

    def own_forward(b, side):
        source = lax.rem(x + (3 if side == 0 else 1), 4)
        rows = ds(source * ROWS + side * (ROWS // 2), ROWS // 2, ROWS // 2)
        return send(
            g_own.at[rows, cols(b)], g_own.at[rows, cols(b)], xf_s.at[b, side], xf_r.at[b, side], sides[side]
        )

    def pair_send(j, s):
        i = j * 2 + s
        return send(
            go.at[:, cols(block_of(j, s + 2))], g_pair.at[ds(x * ROWS, ROWS, ROWS), cols(i)],
            pp_s.at[i], pp_r.at[i], pair,
        )

    def pair_cols(j):
        return ds(j * 2 * BLK, 2 * BLK, 2 * BLK)

    def pair_direct(j, side):
        view = g_pair.at[ds(x * ROWS, ROWS, ROWS), pair_cols(j)]
        return send(view, view, px_s.at[j, side], px_r.at[j, side], sides[side])

    def pair_forward(j, side):
        source = lax.rem(x + (3 if side == 0 else 1), 4)
        view = g_pair.at[ds(source * ROWS + side * (ROWS // 2), ROWS // 2, ROWS // 2), pair_cols(j)]
        return send(view, view, pf_s.at[j, side], pf_r.at[j, side], sides[side])

    def own_start(j, first):
        for s in (first, first + 1):
            for side in (0, 1):
                own_direct(block_of(j, s), side).start()

    def own_pass(j, first):
        for s in (first, first + 1):
            b = block_of(j, s)
            for side in (0, 1):
                own_direct(b, side).wait_recv()
                own_forward(b, side).start()

    def own_end(j, first):
        for s in (first, first + 1):
            for side in (0, 1):
                own_forward(block_of(j, s), side).wait_recv()

    def in_copy(k, src, dst, sem):
        f = ds(k * FC, FC, FC)
        return pltpu.make_async_copy(src.at[:, f], dst.at[:, f], sem.at[k])

    def hid_view(group, half, k):
        return hid.at[ds(group * TOK + half * HALF, HALF, HALF), ds(k * FC, FC, FC)]

    def hid_core(k):
        return send(hid_view(0, c, k), hid_view(0, c, k), hc_s.at[k], hc_r.at[k], core)

    def hid_pair(k):
        return send(hid_view(0, c, k), hid_view(1, c, k), hp_s.at[k], hp_r.at[k], pair)

    def hid_pass(k):
        return send(hid_view(1, c, k), hid_view(1, c, k), hf_s.at[k], hf_r.at[k], core)

    def make_hidden(k):
        in_copy(k, gate, gate_v, ld_g).wait()
        in_copy(k, up, up_v, ld_u).wait()
        f = ds(k * FC, FC, FC)

        def rows(i, carry):
            r = ds(i * STEP, STEP, STEP)
            g = gate_v[r, f].astype(F32)
            u = up_v[r, f].astype(F32)
            hid[ds(c * HALF + i * STEP, STEP, STEP), f] = (g * (1.0 / (1.0 + jnp.exp(-g))) * u).astype(BF16)
            return carry

        lax.fori_loop(0, HALF // STEP, rows, 0)
        hid_pair(k).start()
        hid_core(k).start()

    def dot(rows, k, part):
        return jnp.dot(rows, hid[:, ds(k * FC + part * HF, HF, HF)], preferred_element_type=F32)

    def of_layer(j):
        return g_t[2 * BLK * j : 2 * BLK * (j + 1), :]

    def of_column(s, h):
        return jnp.concatenate(
            [g_t[(4 * h + s) * BLK : (4 * h + s + 1) * BLK, :], g_t[(4 * h + 2 + s) * BLK : (4 * h + 3 + s) * BLK, :]], 0
        )

    def z0(k, half):
        return send(zs0.at[k, half], zr0.at[k, half], z0_s.at[k, half], z0_r.at[k, half], (below, above)[half])

    def z1(k, way):
        return send(zs1.at[k, way], zr1.at[k, way], z1_s.at[k, way], z1_r.at[k, way], (above, below)[way])

    def z_last(k):
        return send(es.at[k], er.at[k], e_s.at[k], e_r.at[k], across)

    def y_first(k):
        return send(as_.at[k], ar.at[k], a_s.at[k], a_r.at[k], across)

    def y0(k, half):
        return send(ys0.at[k, half], yr0.at[k, half], y0_s.at[k, half], y0_r.at[k, half], (below, above)[half])

    def y1(k, way):
        return send(ys1.at[k, way], yr1.at[k, way], y1_s.at[k, way], y1_r.at[k, way], (above, below)[way])

    def stage0(k):
        part = dot(of_layer(0), k, 1).astype(BF16)
        for half in (0, 1):
            zs0[k, half] = part[:, half * BLK : (half + 1) * BLK]
            z0(k, half).start()
        for h in (0, 1):
            as_[k, 2 * BLK * h : 2 * BLK * (h + 1), :] = dot(of_column(1, h), k, 0).astype(BF16)
        y_first(k).start()

    def stage1(k):
        for way in (0, 1):
            part = dot(of_layer(1 + way), k, 1)
            half = 1 - way
            z0(k, half).wait_recv()
            lo, hi = part[:, :BLK], part[:, BLK:]
            got = zr0[k, half].astype(F32)
            if half:
                hi = hi + got
            else:
                lo = lo + got
            zs1[k, way, :, :BLK] = lo.astype(BF16)
            zs1[k, way, :, BLK:] = hi.astype(BF16)
            z1(k, way).start()
        parts = [dot(of_column(0, h), k, 0) for h in (0, 1)]
        y_first(k).wait_recv()
        first = parts[0] + ar[k, : 2 * BLK, :].astype(F32)
        far = first[:BLK, :].astype(BF16)
        for half in (0, 1):
            ys0[k, half] = far[:, half * BLK : (half + 1) * BLK]
            y0(k, half).start()
        ykeep[k, :BLK, :] = first[BLK:, :]
        ykeep[k, BLK:, :] = parts[1] + ar[k, 2 * BLK :, :].astype(F32)

    def stage2(k):
        for way in (0, 1):
            half = 1 - way
            y0(k, half).wait_recv()
            got = yr0[k, half].astype(F32)
            lo, hi = ykeep[k, BLK * way : BLK * (way + 1), :BLK], ykeep[k, BLK * way : BLK * (way + 1), BLK:]
            if half:
                hi = hi + got
            else:
                lo = lo + got
            ys1[k, way, :, :BLK] = lo.astype(BF16)
            ys1[k, way, :, BLK:] = hi.astype(BF16)
            y1(k, way).start()
        part = dot(of_layer(3), k, 1)
        for way in (0, 1):
            z1(k, way).wait_recv()
            part = part + zr1[k, way].astype(F32)
        es[k] = part[BLK:, :].astype(BF16)
        z_last(k).start()
        zkeep[k] = part[:BLK, :]

    def out_copy(k):
        f = ds(k * FC, FC, FC)
        return pltpu.make_async_copy(wout.at[f], o_w.at[f], st_w.at[k])

    def stage3(k):
        total = ykeep[k, 2 * BLK :, :]
        for way in (0, 1):
            y1(k, way).wait_recv()
            total = total + yr1[k, way].astype(F32)
        wout[ds(k * FC, HF, HF), :] = (total * SCALE).T.astype(BF16)
        z_last(k).wait_recv()
        total = zkeep[k] + er[k].astype(F32)
        wout[ds(k * FC + HF, HF, HF), :] = (total * SCALE).T.astype(BF16)
        out_copy(k).start()

    def w_copy(k):
        slot = lax.rem(k, 2)
        return pltpu.make_async_copy(w.at[ds(k * FC, FC, FC)], wbuf.at[slot], ld_w.at[slot])

    def gh_send(k):
        return send(ghs.at[k, ds((1 - c) * HALF, HALF, HALF)], ghr.at[k], gh_s.at[k], gh_r.at[k], core)

    def grad_hidden(k):
        w_copy(k).wait()

        def tile(n, carry):
            f = ds(n * HF, HF, HF)
            ghs[k, :, f] = lax.dot_general(
                g_own[...], wbuf[lax.rem(k, 2), f, :], (((1,), (1,)), ((), ())), preferred_element_type=F32
            ).astype(BF16)
            return carry

        lax.fori_loop(0, 2, tile, 0)
        gh_send(k).start()

        @pl.when(k + 2 < NC)
        def _():
            w_copy(k + 2).start()

    def gate_out(k):
        f = ds(k * FC, FC, FC)
        return (
            pltpu.make_async_copy(gate_v.at[:, f], o_gate.at[:, f], st_g.at[k]),
            pltpu.make_async_copy(up_v.at[:, f], o_up.at[:, f], st_u.at[k]),
        )

    def grad_gate(k):
        gh_send(k).wait_recv()
        f = ds(k * FC, FC, FC)

        def rows(i, carry):
            r = ds(i * STEP, STEP, STEP)
            g = gate_v[r, f].astype(F32)
            u = up_v[r, f].astype(F32)
            grad = ghs[k, ds(c * HALF + i * STEP, STEP, STEP), :].astype(F32) + ghr[k, r, :].astype(F32)
            sig = 1.0 / (1.0 + jnp.exp(-g))
            gate_v[r, f] = (grad * u * (sig * (1.0 + g * (1.0 - sig)))).astype(BF16)
            up_v[r, f] = (grad * (g * sig)).astype(BF16)
            return carry

        lax.fori_loop(0, HALF // STEP, rows, 0)
        for copy in gate_out(k):
            copy.start()

    def loads(k, carry):
        in_copy(k, gate, gate_v, ld_g).start()
        in_copy(k, up, up_v, ld_u).start()
        return carry

    own_start(0, 0)
    for s in (0, 1):
        pair_send(0, s).start()
    lax.fori_loop(0, NC, loads, 0)
    own_copy().start()
    w_copy(0).start()
    w_copy(1).start()

    def first_hidden(k, carry):
        make_hidden(k)

        @pl.when(k == 0)
        def _():
            for j in (1, 2, 3):
                for s in (0, 1):
                    pair_send(j, s).start()

        return carry

    lax.fori_loop(0, 2, first_hidden, 0)
    own_copy().wait()

    def gather(j, carry):
        @pl.when(j < 3)
        def _():
            own_start(j + 1, 0)

        for s in (0, 1):
            pair_send(j, s).wait_recv()
        for side in (0, 1):
            pair_direct(j, side).start()
        own_pass(j, 0)
        for side in (0, 1):
            pair_direct(j, side).wait_recv()
            pair_forward(j, side).start()

        @pl.when(j == 3)
        def _():
            def rest(i, carry):
                own_start(i, 2)
                return carry

            lax.fori_loop(0, 4, rest, 0)

        own_end(j, 0)
        for side in (0, 1):
            pair_forward(j, side).wait_recv()
        for s in (0, 1):
            rows = ds((j * 2 + s) * BLK, BLK, BLK)
            g_t[rows, :TOK] = g_own[:, cols(block_of(j, s))].T
            g_t[rows, TOK:] = g_pair[:, cols(j * 2 + s)].T
        return carry

    lax.fori_loop(0, 4, gather, 0)
    hid_pair(0).wait_recv()
    hid_pass(0).start()

    def body(i, carry):
        @pl.when(i + 2 < NC)
        def _():
            make_hidden(i + 2)

        @pl.when(i < NC)
        def _():
            hid_core(i).wait_recv()
            hid_pass(i).wait_recv()
            stage0(i)

        @pl.when(jnp.logical_and(i >= 1, i < NC + 1))
        def _():
            stage1(i - 1)

        @pl.when(jnp.logical_and(i >= 2, i < NC + 2))
        def _():
            stage2(i - 2)

        @pl.when(jnp.logical_and(i >= 3, i < NC + 3))
        def _():
            stage3(i - 3)

        @pl.when(i < 4)
        def _():
            own_pass(i, 2)

        @pl.when(i == 3)
        def _():
            def rest(j, carry):
                own_end(j, 2)
                return carry

            lax.fori_loop(0, 4, rest, 0)

        @pl.when(jnp.logical_and(i >= 3, i < NC + 3))
        def _():
            grad_hidden(i - 3)

        @pl.when(i >= 4)
        def _():
            grad_gate(i - 4)

        @pl.when(i + 1 < NC)
        def _():
            hid_pair(i + 1).wait_recv()
            hid_pass(i + 1).start()

        return carry

    lax.fori_loop(0, NC + 4, body, 0)

    def sent(k, carry):
        hid_core(k).wait_send()
        hid_pair(k).wait_send()
        hid_pass(k).wait_send()
        for i in (0, 1):
            z0(k, i).wait_send()
            z1(k, i).wait_send()
            y0(k, i).wait_send()
            y1(k, i).wait_send()
        z_last(k).wait_send()
        y_first(k).wait_send()
        gh_send(k).wait_send()
        for copy in gate_out(k):
            copy.wait()
        out_copy(k).wait()
        return carry

    lax.fori_loop(0, NC, sent, 0)

    def sent_x(j, carry):
        for s in range(4):
            for side in (0, 1):
                own_direct(block_of(j, s), side).wait_send()
                own_forward(block_of(j, s), side).wait_send()
        for s in (0, 1):
            pair_send(j, s).wait_send()
        for side in (0, 1):
            pair_direct(j, side).wait_send()
            pair_forward(j, side).wait_send()
        return carry

    lax.fori_loop(0, 4, sent_x, 0)


def on_device(grad_out, gate_pre, up_pre, down_weight):
    dma = pltpu.SemaphoreType.DMA
    vmem = lambda *shape: pltpu.VMEM(shape, BF16)
    scratch = [
        vmem(TOK, DM), vmem(TOK, 8 * BLK), vmem(8 * BLK, 2 * TOK), vmem(2 * TOK, FF),
        vmem(HALF, FF), vmem(HALF, FF), vmem(2, FC, DM), vmem(NC, TOK, FC), vmem(NC, HALF, FC), vmem(FF, BLK),
        vmem(NC, 2, 2 * BLK, BLK), vmem(NC, 2, 2 * BLK, BLK), vmem(NC, 2, 2 * BLK, HF), vmem(NC, 2, 2 * BLK, HF),
        vmem(NC, BLK, HF), vmem(NC, BLK, HF), pltpu.VMEM((NC, BLK, HF), F32),
        vmem(NC, 4 * BLK, HF), vmem(NC, 4 * BLK, HF), vmem(NC, 2, BLK, BLK), vmem(NC, 2, BLK, BLK),
        vmem(NC, 2, BLK, HF), vmem(NC, 2, BLK, HF), pltpu.VMEM((NC, 3 * BLK, HF), F32),
        dma((16, 2)), dma((16, 2)), dma((16, 2)), dma((16, 2)), dma((8,)), dma((8,)),
        dma((4, 2)), dma((4, 2)), dma((4, 2)), dma((4, 2)),
        dma((NC,)), dma((NC,)), dma((NC,)), dma((NC,)), dma((NC,)), dma((NC,)),
        dma((NC, 2)), dma((NC, 2)), dma((NC, 2)), dma((NC, 2)), dma((NC,)), dma((NC,)),
        dma((NC,)), dma((NC,)), dma((NC, 2)), dma((NC, 2)), dma((NC, 2)), dma((NC, 2)),
        dma((NC,)), dma((NC,)), dma((NC,)), dma((NC,)), dma, dma((2,)), dma((NC,)), dma((NC,)), dma((NC,)),
    ]
    anywhere = pl.BlockSpec(memory_space=pl.ANY)
    grad_gate, grad_up, grad_weight = pl.pallas_call(
        kernel,
        out_shape=(
            jax.ShapeDtypeStruct((HALF, FF), BF16),
            jax.ShapeDtypeStruct((HALF, FF), BF16),
            jax.ShapeDtypeStruct((FF, BLK), BF16),
        ),
        in_specs=[anywhere] * 4,
        out_specs=(anywhere,) * 3,
        scratch_shapes=scratch,
        compiler_params=pltpu.CompilerParams(
            collective_id=0, has_side_effects=True, vmem_limit_bytes=60 * 2**20
        ),
        cost_estimate=pl.CostEstimate(flops=4 * TOK * FF * DM, bytes_accessed=24 * 10**6, transcendentals=2 * HALF * FF),
    )(grad_out[0], gate_pre[0], up_pre[0], down_weight)
    return grad_gate[None], grad_up[None], grad_weight


def solution(mesh):
    in_specs = (
        P("depth", "row", "col"),
        P("depth", "col", "row"),
        P("depth", "col", "row"),
        P("row", "col"),
    )
    out_specs = (P("depth", "col", "row"), P("depth", "col", "row"), P("row", ("col", "depth")))
    return jax.shard_map(
        on_device, mesh=mesh, in_specs=in_specs, out_specs=out_specs, check_vma=False
    )
```

```python
import jax
import jax.numpy as jnp
from jax import lax
from jax.experimental import pallas as pl
from jax.experimental.pallas import tpu as pltpu
from jax.sharding import PartitionSpec as P

MESH = pl.DeviceIdType.MESH
BF16, F32 = jnp.bfloat16, jnp.float32

TOK, FF, DM = 512, 3584, 2048
HALF = TOK // 2
ROWS = TOK // 4
FC = 512
NC = FF // FC
HF = FC // 2
NU = FF // HF
NY = 6
NZ = NU - NY
BLK = 128
STEP = 32
SCALE = float(16 * TOK) ** -0.5


def kernel(
    go, gate, up, w, gate_v, up_v, wout,
    g_own, g_pair, g_t, hid, wbuf, ghs, ghr,
    zs0, zr0, zs1, zr1, es, er, zkeep,
    as_, ar, ys0, yr0, ys1, yr1, ykeep,
    xo_s, xo_r, xf_s, xf_r, pp_s, pp_r, px_s, px_r, pf_s, pf_r,
    hc_s, hc_r, hp_s, hp_r, hf_s, hf_r,
    z0_s, z0_r, z1_s, z1_r, e_s, e_r, a_s, a_r, y0_s, y0_r, y1_s, y1_r,
    gh_s, gh_r, ld_g, ld_u, ld_o, ld_w,
):
    x, c, q = lax.axis_index("row"), lax.axis_index("col"), lax.axis_index("depth")
    z, y = lax.div(q, 4), lax.rem(q, 4)
    odd = lax.rem(y, 2)
    y_pair = y + 1 - 2 * odd
    y_sum = lax.rem(y + 3 + 2 * odd, 4)
    y_pair_sum = lax.rem(y_pair + 3 + 2 * (1 - odd), 4)
    core = (x, 1 - c, q)
    right, left = (lax.rem(x + 1, 4), c, q), (lax.rem(x + 3, 4), c, q)
    sides = (right, left)
    pair = (x, c, z * 4 + y_pair)
    across = (x, c, z * 4 + y_sum)
    above, below = (x, c, lax.rem(z + 1, 4) * 4 + y), (x, c, lax.rem(z + 3, 4) * 4 + y)

    barrier = pltpu.get_barrier_semaphore()
    for other in (core, right, left, pair, across, above, below):
        pl.semaphore_signal(barrier, inc=1, device_id=other, device_id_type=MESH)
    pl.semaphore_wait(barrier, 7)

    def send(src, dst, ss, rs, device):
        return pltpu.make_async_remote_copy(
            src_ref=src, dst_ref=dst, send_sem=ss, recv_sem=rs, device_id=device, device_id_type=MESH
        )

    def ds(start, size, unit):
        return pl.ds(pl.multiple_of(start, unit), size)

    def layer(j):
        return lax.rem(z + jnp.where(j == 0, 2, jnp.where(j == 1, 1, jnp.where(j == 2, 3, 0))), 4)

    def block_of(j, s):
        column = (y, y_sum, y_pair, y_pair_sum)[s]
        return layer(j) * 4 + column

    def cols(b):
        return ds(b * BLK, BLK, BLK)

    def own_copy():
        return pltpu.make_async_copy(go, g_own.at[ds(x * ROWS, ROWS, ROWS)], ld_o)

    def own_direct(b, side):
        return send(
            go.at[:, cols(b)], g_own.at[ds(x * ROWS, ROWS, ROWS), cols(b)],
            xo_s.at[b, side], xo_r.at[b, side], sides[side],
        )

    def own_forward(b, side):
        source = lax.rem(x + (3 if side == 0 else 1), 4)
        rows = ds(source * ROWS + side * (ROWS // 2), ROWS // 2, ROWS // 2)
        return send(
            g_own.at[rows, cols(b)], g_own.at[rows, cols(b)], xf_s.at[b, side], xf_r.at[b, side], sides[side]
        )

    def pair_send(j, s):
        i = j * 2 + s
        return send(
            go.at[:, cols(block_of(j, s + 2))], g_pair.at[ds(x * ROWS, ROWS, ROWS), cols(i)],
            pp_s.at[i], pp_r.at[i], pair,
        )

    def pair_cols(j):
        return ds(j * 2 * BLK, 2 * BLK, 2 * BLK)

    def pair_direct(j, side):
        view = g_pair.at[ds(x * ROWS, ROWS, ROWS), pair_cols(j)]
        return send(view, view, px_s.at[j, side], px_r.at[j, side], sides[side])

    def pair_forward(j, side):
        source = lax.rem(x + (3 if side == 0 else 1), 4)
        view = g_pair.at[ds(source * ROWS + side * (ROWS // 2), ROWS // 2, ROWS // 2), pair_cols(j)]
        return send(view, view, pf_s.at[j, side], pf_r.at[j, side], sides[side])

    def own_start(j, first):
        for s in (first, first + 1):
            for side in (0, 1):
                own_direct(block_of(j, s), side).start()

    def own_pass(j, first):
        for s in (first, first + 1):
            b = block_of(j, s)
            for side in (0, 1):
                own_direct(b, side).wait_recv()
                own_forward(b, side).start()

    def own_end(j, first):
        for s in (first, first + 1):
            for side in (0, 1):
                own_forward(block_of(j, s), side).wait_recv()

    def in_copy(k, src, dst, sem):
        f = ds(k * FC, FC, FC)
        return pltpu.make_async_copy(src.at[:, f], dst.at[:, f], sem.at[k])

    def hid_view(group, u):
        return hid.at[ds(group * TOK + c * HALF, HALF, HALF), ds(u * HF, HF, HF)]

    def hid_core(u):
        return send(hid_view(0, u), hid_view(0, u), hc_s.at[u], hc_r.at[u], core)

    def hid_pair(u):
        return send(hid_view(0, u), hid_view(1, u), hp_s.at[u], hp_r.at[u], pair)

    def hid_pass(u):
        return send(hid_view(1, u), hid_view(1, u), hf_s.at[u], hf_r.at[u], core)

    def pass_on(u):
        hid_pair(u).wait_recv()
        hid_pass(u).start()

    def have_hidden(u):
        hid_core(u).wait_recv()
        hid_pass(u).wait_recv()

    def make_hidden(k):
        in_copy(k, gate, gate_v, ld_g).wait()
        in_copy(k, up, up_v, ld_u).wait()
        f = ds(k * FC, FC, FC)

        def rows(i, carry):
            r = ds(i * STEP, STEP, STEP)
            g = gate_v[r, f].astype(F32)
            u = up_v[r, f].astype(F32)
            hid[ds(c * HALF + i * STEP, STEP, STEP), f] = (g * (1.0 / (1.0 + jnp.exp(-g))) * u).astype(BF16)
            return carry

        lax.fori_loop(0, HALF // STEP, rows, 0)
        for u in (2 * k, 2 * k + 1):
            hid_pair(u).start()
            hid_core(u).start()

    def dot(rows, u):
        return jnp.dot(rows, hid[:, ds(u * HF, HF, HF)], preferred_element_type=F32)

    def unit_z(k):
        return jnp.maximum(2 * k - 1, 0)

    def unit_y(k):
        return 2 * k + 2

    def of_layer(j):
        return g_t[2 * BLK * j : 2 * BLK * (j + 1), :]

    def of_column(s, h):
        return jnp.concatenate(
            [g_t[(4 * h + s) * BLK : (4 * h + s + 1) * BLK, :], g_t[(4 * h + 2 + s) * BLK : (4 * h + 3 + s) * BLK, :]], 0
        )

    def z0(k, half):
        return send(zs0.at[k, half], zr0.at[k, half], z0_s.at[k, half], z0_r.at[k, half], (below, above)[half])

    def z1(k, way):
        return send(zs1.at[k, way], zr1.at[k, way], z1_s.at[k, way], z1_r.at[k, way], (above, below)[way])

    def z_last(k):
        return send(es.at[k], er.at[k], e_s.at[k], e_r.at[k], across)

    def y_first(k):
        return send(as_.at[k], ar.at[k], a_s.at[k], a_r.at[k], across)

    def y0(k, half):
        return send(ys0.at[k, half], yr0.at[k, half], y0_s.at[k, half], y0_r.at[k, half], (below, above)[half])

    def y1(k, way):
        return send(ys1.at[k, way], yr1.at[k, way], y1_s.at[k, way], y1_r.at[k, way], (above, below)[way])

    def z_stage0(k):
        part = dot(of_layer(0), unit_z(k)).astype(BF16)
        for half in (0, 1):
            zs0[k, half] = part[:, half * BLK : (half + 1) * BLK]
            z0(k, half).start()

    def y_stage0(k):
        for h in (0, 1):
            as_[k, 2 * BLK * h : 2 * BLK * (h + 1), :] = dot(of_column(1, h), unit_y(k)).astype(BF16)
        y_first(k).start()

    def z_stage1(k):
        for way in (0, 1):
            part = dot(of_layer(1 + way), unit_z(k))
            half = 1 - way
            z0(k, half).wait_recv()
            lo, hi = part[:, :BLK], part[:, BLK:]
            got = zr0[k, half].astype(F32)
            if half:
                hi = hi + got
            else:
                lo = lo + got
            zs1[k, way, :, :BLK] = lo.astype(BF16)
            zs1[k, way, :, BLK:] = hi.astype(BF16)
            z1(k, way).start()

    def y_stage1(k):
        parts = [dot(of_column(0, h), unit_y(k)) for h in (0, 1)]
        y_first(k).wait_recv()
        first = parts[0] + ar[k, : 2 * BLK, :].astype(F32)
        far = first[:BLK, :].astype(BF16)
        for half in (0, 1):
            ys0[k, half] = far[:, half * BLK : (half + 1) * BLK]
            y0(k, half).start()
        ykeep[k, :BLK, :] = first[BLK:, :]
        ykeep[k, BLK:, :] = parts[1] + ar[k, 2 * BLK :, :].astype(F32)

    def z_stage2(k):
        part = dot(of_layer(3), unit_z(k))
        for way in (0, 1):
            z1(k, way).wait_recv()
            part = part + zr1[k, way].astype(F32)
        es[k] = part[BLK:, :].astype(BF16)
        z_last(k).start()
        zkeep[k] = part[:BLK, :]

    def y_stage2(k):
        for way in (0, 1):
            half = 1 - way
            y0(k, half).wait_recv()
            got = yr0[k, half].astype(F32)
            lo, hi = ykeep[k, BLK * way : BLK * (way + 1), :BLK], ykeep[k, BLK * way : BLK * (way + 1), BLK:]
            if half:
                hi = hi + got
            else:
                lo = lo + got
            ys1[k, way, :, :BLK] = lo.astype(BF16)
            ys1[k, way, :, BLK:] = hi.astype(BF16)
            y1(k, way).start()

    def z_stage3(k):
        z_last(k).wait_recv()
        total = zkeep[k] + er[k].astype(F32)
        wout[ds(unit_z(k) * HF, HF, HF), :] = (total * SCALE).T.astype(BF16)

    def y_stage3(k):
        total = ykeep[k, 2 * BLK :, :]
        for way in (0, 1):
            y1(k, way).wait_recv()
            total = total + yr1[k, way].astype(F32)
        wout[ds(unit_y(k) * HF, HF, HF), :] = (total * SCALE).T.astype(BF16)

    def w_copy(k):
        slot = lax.rem(k, 2)
        return pltpu.make_async_copy(w.at[ds(k * FC, FC, FC)], wbuf.at[slot], ld_w.at[slot])

    def gh_send(k):
        return send(ghs.at[k, ds((1 - c) * HALF, HALF, HALF)], ghr.at[k], gh_s.at[k], gh_r.at[k], core)

    def grad_hidden(k):
        w_copy(k).wait()

        def tile(n, carry):
            f = ds(n * HF, HF, HF)
            ghs[k, :, f] = lax.dot_general(
                g_own[...], wbuf[lax.rem(k, 2), f, :], (((1,), (1,)), ((), ())), preferred_element_type=F32
            ).astype(BF16)
            return carry

        lax.fori_loop(0, 2, tile, 0)
        gh_send(k).start()

        @pl.when(k + 2 < NC)
        def _():
            w_copy(k + 2).start()

    def grad_gate(k):
        gh_send(k).wait_recv()
        f = ds(k * FC, FC, FC)

        def rows(i, carry):
            r = ds(i * STEP, STEP, STEP)
            g = gate_v[r, f].astype(F32)
            u = up_v[r, f].astype(F32)
            grad = ghs[k, ds(c * HALF + i * STEP, STEP, STEP), :].astype(F32) + ghr[k, r, :].astype(F32)
            sig = 1.0 / (1.0 + jnp.exp(-g))
            gate_v[r, f] = (grad * u * (sig * (1.0 + g * (1.0 - sig)))).astype(BF16)
            up_v[r, f] = (grad * (g * sig)).astype(BF16)
            return carry

        lax.fori_loop(0, HALF // STEP, rows, 0)

    def loop(lo, hi, step):
        def run(i, carry):
            step(i)
            return carry

        lax.fori_loop(lo, hi, run, 0)

    def load(k):
        in_copy(k, gate, gate_v, ld_g).start()
        in_copy(k, up, up_v, ld_u).start()

    def pair_start(j):
        for s in (0, 1):
            pair_send(j, s).start()

    own_start(0, 0)
    own_start(1, 0)
    pair_start(0)
    pair_start(1)
    loop(0, NC, load)
    own_copy().start()
    w_copy(0).start()
    w_copy(1).start()

    def first_hidden(k):
        make_hidden(k)

        @pl.when(k == 0)
        def _():
            pair_start(2)
            pair_start(3)

    loop(0, 3, first_hidden)

    def gather(t):
        @pl.when(t < 4)
        def _():
            own_pass(t, 0)
            for s in (0, 1):
                pair_send(t, s).wait_recv()
            for side in (0, 1):
                pair_direct(t, side).start()

        @pl.when(t < 2)
        def _():
            own_start(t + 2, 0)

        @pl.when(t >= 1)
        def _():
            for side in (0, 1):
                pair_direct(t - 1, side).wait_recv()
                pair_forward(t - 1, side).start()

        @pl.when(t < 4)
        def _():
            make_hidden(t + 3)

    loop(0, 5, gather)
    loop(0, 4, lambda j: own_start(j, 2))
    own_copy().wait()

    def turn(j):
        own_end(j, 0)
        for side in (0, 1):
            pair_forward(j, side).wait_recv()
        for s in (0, 1):
            rows = ds((j * 2 + s) * BLK, BLK, BLK)
            g_t[rows, :TOK] = g_own[:, cols(block_of(j, s))].T
            g_t[rows, TOK:] = g_pair[:, cols(j * 2 + s)].T

        @pl.when(j < 2)
        def _():
            pass_on(j)
            have_hidden(j)
            z_stage0(j)

        @pl.when(j == 2)
        def _():
            z_stage1(0)

    loop(0, 4, turn)

    def body(i):
        @pl.when(i < NC)
        def _():
            pass_on(2 * i)
            have_hidden(2 * i)
            y_stage0(i - 1)
            pass_on(2 * i + 1)
            have_hidden(2 * i + 1)
            z_stage0(i + 1)

        @pl.when(i < NZ)
        def _():
            z_stage1(i)

        @pl.when(jnp.logical_and(i >= 2, i < NY + 2))
        def _():
            y_stage1(i - 2)

        @pl.when(i < NZ + 1)
        def _():
            z_stage2(i - 1)

        @pl.when(jnp.logical_and(i >= 3, i < NY + 3))
        def _():
            y_stage2(i - 3)

        @pl.when(jnp.logical_and(i >= 2, i < NZ + 2))
        def _():
            z_stage3(i - 2)

        @pl.when(jnp.logical_and(i >= 4, i < NY + 4))
        def _():
            y_stage3(i - 4)

        @pl.when(i == 1)
        def _():
            loop(0, 4, lambda j: own_pass(j, 2))

        @pl.when(i == 2)
        def _():
            loop(0, 4, lambda j: own_end(j, 2))

        def products(d):
            k = 2 * i - 5 + d

            @pl.when(jnp.logical_and(k >= 0, k < NC))
            def _():
                grad_hidden(k)

            @pl.when(jnp.logical_and(k >= 2, k < NC + 2))
            def _():
                grad_gate(k - 2)

        loop(0, 2, products)

    loop(1, NZ + 2, body)

    def sent(u):
        hid_core(u).wait_send()
        hid_pair(u).wait_send()
        hid_pass(u).wait_send()

    def sent_z(k):
        for i in (0, 1):
            z0(k, i).wait_send()
            z1(k, i).wait_send()
        z_last(k).wait_send()

    def sent_y(k):
        for i in (0, 1):
            y0(k, i).wait_send()
            y1(k, i).wait_send()
        y_first(k).wait_send()

    def sent_x(j):
        for s in range(4):
            for side in (0, 1):
                own_direct(block_of(j, s), side).wait_send()
                own_forward(block_of(j, s), side).wait_send()
        for s in (0, 1):
            pair_send(j, s).wait_send()
        for side in (0, 1):
            pair_direct(j, side).wait_send()
            pair_forward(j, side).wait_send()

    loop(0, NU, sent)
    loop(0, NZ, sent_z)
    loop(0, NY, sent_y)
    loop(0, NC, lambda k: gh_send(k).wait_send())
    loop(0, 4, sent_x)


def on_device(grad_out, gate_pre, up_pre, down_weight):
    dma = pltpu.SemaphoreType.DMA
    vmem = lambda *shape: pltpu.VMEM(shape, BF16)
    scratch = [
        vmem(TOK, DM), vmem(TOK, 8 * BLK), vmem(8 * BLK, 2 * TOK), vmem(2 * TOK, FF),
        vmem(2, FC, DM), vmem(NC, TOK, FC), vmem(NC, HALF, FC),
        vmem(NZ, 2, 2 * BLK, BLK), vmem(NZ, 2, 2 * BLK, BLK), vmem(NZ, 2, 2 * BLK, HF), vmem(NZ, 2, 2 * BLK, HF),
        vmem(NZ, BLK, HF), vmem(NZ, BLK, HF), pltpu.VMEM((NZ, BLK, HF), F32),
        vmem(NY, 4 * BLK, HF), vmem(NY, 4 * BLK, HF), vmem(NY, 2, BLK, BLK), vmem(NY, 2, BLK, BLK),
        vmem(NY, 2, BLK, HF), vmem(NY, 2, BLK, HF), pltpu.VMEM((NY, 3 * BLK, HF), F32),
        dma((16, 2)), dma((16, 2)), dma((16, 2)), dma((16, 2)), dma((8,)), dma((8,)),
        dma((4, 2)), dma((4, 2)), dma((4, 2)), dma((4, 2)),
        dma((NU,)), dma((NU,)), dma((NU,)), dma((NU,)), dma((NU,)), dma((NU,)),
        dma((NZ, 2)), dma((NZ, 2)), dma((NZ, 2)), dma((NZ, 2)), dma((NZ,)), dma((NZ,)),
        dma((NY,)), dma((NY,)), dma((NY, 2)), dma((NY, 2)), dma((NY, 2)), dma((NY, 2)),
        dma((NC,)), dma((NC,)), dma((NC,)), dma((NC,)), dma, dma((2,)),
    ]
    anywhere = pl.BlockSpec(memory_space=pl.ANY)
    grad_gate, grad_up, grad_weight = pl.pallas_call(
        kernel,
        out_shape=(pltpu.VMEM((HALF, FF), BF16), pltpu.VMEM((HALF, FF), BF16), pltpu.VMEM((FF, BLK), BF16)),
        in_specs=[anywhere] * 4,
        out_specs=(pl.BlockSpec(memory_space=pltpu.VMEM),) * 3,
        scratch_shapes=scratch,
        compiler_params=pltpu.CompilerParams(
            collective_id=0, has_side_effects=True, vmem_limit_bytes=48 * 2**20
        ),
        cost_estimate=pl.CostEstimate(flops=4 * TOK * FF * DM, bytes_accessed=24 * 10**6, transcendentals=2 * HALF * FF),
    )(grad_out[0], gate_pre[0], up_pre[0], down_weight)
    return grad_gate[None], grad_up[None], grad_weight


def solution(mesh):
    in_specs = (
        P("depth", "row", "col"),
        P("depth", "col", "row"),
        P("depth", "col", "row"),
        P("row", "col"),
    )
    out_specs = (P("depth", "col", "row"), P("depth", "col", "row"), P("row", ("col", "depth")))
    return jax.shard_map(
        on_device, mesh=mesh, in_specs=in_specs, out_specs=out_specs, check_vma=False
    )
```

```python
import jax
import jax.numpy as jnp
from jax import lax
from jax.experimental import pallas as pl
from jax.experimental.pallas import tpu as pltpu
from jax.sharding import PartitionSpec as P

MESH = pl.DeviceIdType.MESH
BF16, F32 = jnp.bfloat16, jnp.float32

TOK, FF, DM = 512, 3584, 2048
HALF = TOK // 2
ROWS = TOK // 4
FC = 512
NC = FF // FC
HF = FC // 2
NU = FF // HF
NY = 5
NZ = NU - NY
BLK = 128
STEP = 32
SCALE = float(16 * TOK) ** -0.5


def sigmoid(v):
    return 0.5 * jnp.tanh(0.5 * v) + 0.5


def kernel(
    go, gate, up, w, gate_v, up_v, wout,
    g_own, g_pair, g_t, hid, wbuf, ghs, ghr,
    zs0, zr0, zs1, zr1, es, er, zkeep,
    as_, ar, ys0, yr0, ys1, yr1, ykeep,
    xo_s, xo_r, xf_s, xf_r, pp_s, pp_r, px_s, px_r, pf_s, pf_r,
    hc_s, hc_r, hp_s, hp_r, hf_s, hf_r,
    z0_s, z0_r, z1_s, z1_r, e_s, e_r, a_s, a_r, y0_s, y0_r, y1_s, y1_r,
    gh_s, gh_r, ld_g, ld_u, ld_o, ld_w,
):
    x, c, q = lax.axis_index("row"), lax.axis_index("col"), lax.axis_index("depth")
    z, y = lax.div(q, 4), lax.rem(q, 4)
    odd = lax.rem(y, 2)
    y_pair = y + 1 - 2 * odd
    y_sum = lax.rem(y + 3 + 2 * odd, 4)
    y_pair_sum = lax.rem(y_pair + 3 + 2 * (1 - odd), 4)
    core = (x, 1 - c, q)
    right, left = (lax.rem(x + 1, 4), c, q), (lax.rem(x + 3, 4), c, q)
    sides = (right, left)
    pair = (x, c, z * 4 + y_pair)
    across = (x, c, z * 4 + y_sum)
    above, below = (x, c, lax.rem(z + 1, 4) * 4 + y), (x, c, lax.rem(z + 3, 4) * 4 + y)

    barrier = pltpu.get_barrier_semaphore()
    for other in (core, right, left, pair, across, above, below):
        pl.semaphore_signal(barrier, inc=1, device_id=other, device_id_type=MESH)
    def send(src, dst, ss, rs, device):
        return pltpu.make_async_remote_copy(
            src_ref=src, dst_ref=dst, send_sem=ss, recv_sem=rs, device_id=device, device_id_type=MESH
        )

    def ds(start, size, unit):
        return pl.ds(pl.multiple_of(start, unit), size)

    def layer(j):
        return lax.rem(z + jnp.where(j == 0, 2, jnp.where(j == 1, 1, jnp.where(j == 2, 3, 0))), 4)

    def block_of(j, s):
        column = (y, y_sum, y_pair, y_pair_sum)[s]
        return layer(j) * 4 + column

    def cols(b):
        return ds(b * BLK, BLK, BLK)

    def own_copy():
        return pltpu.make_async_copy(go, g_own.at[ds(x * ROWS, ROWS, ROWS)], ld_o)

    def own_direct(b, side):
        return send(
            go.at[:, cols(b)], g_own.at[ds(x * ROWS, ROWS, ROWS), cols(b)],
            xo_s.at[b, side], xo_r.at[b, side], sides[side],
        )

    def own_forward(b, side):
        source = lax.rem(x + (3 if side == 0 else 1), 4)
        rows = ds(source * ROWS + side * (ROWS // 2), ROWS // 2, ROWS // 2)
        return send(
            g_own.at[rows, cols(b)], g_own.at[rows, cols(b)], xf_s.at[b, side], xf_r.at[b, side], sides[side]
        )

    def pair_send(j, s):
        i = j * 2 + s
        return send(
            go.at[:, cols(block_of(j, s + 2))], g_pair.at[ds(x * ROWS, ROWS, ROWS), cols(i)],
            pp_s.at[i], pp_r.at[i], pair,
        )

    def pair_cols(j):
        return ds(j * 2 * BLK, 2 * BLK, 2 * BLK)

    def pair_direct(j, side):
        view = g_pair.at[ds(x * ROWS, ROWS, ROWS), pair_cols(j)]
        return send(view, view, px_s.at[j, side], px_r.at[j, side], sides[side])

    def pair_forward(j, side):
        source = lax.rem(x + (3 if side == 0 else 1), 4)
        view = g_pair.at[ds(source * ROWS + side * (ROWS // 2), ROWS // 2, ROWS // 2), pair_cols(j)]
        return send(view, view, pf_s.at[j, side], pf_r.at[j, side], sides[side])

    def own_start(j, first):
        for s in (first, first + 1):
            for side in (0, 1):
                own_direct(block_of(j, s), side).start()

    def own_pass(j, first):
        for s in (first, first + 1):
            b = block_of(j, s)
            for side in (0, 1):
                own_direct(b, side).wait_recv()
                own_forward(b, side).start()

    def own_end(j, first):
        for s in (first, first + 1):
            for side in (0, 1):
                own_forward(block_of(j, s), side).wait_recv()

    def in_copy(k, src, dst, sem):
        f = ds(k * FC, FC, FC)
        return pltpu.make_async_copy(src.at[:, f], dst.at[:, f], sem.at[k])

    def hid_view(group, u):
        return hid.at[ds(group * TOK + c * HALF, HALF, HALF), ds(u * HF, HF, HF)]

    def hid_core(u):
        return send(hid_view(0, u), hid_view(0, u), hc_s.at[u], hc_r.at[u], core)

    def hid_pair(u):
        return send(hid_view(0, u), hid_view(1, u), hp_s.at[u], hp_r.at[u], pair)

    def hid_pass(u):
        return send(hid_view(1, u), hid_view(1, u), hf_s.at[u], hf_r.at[u], core)

    def pass_on(u):
        hid_pair(u).wait_recv()
        hid_pass(u).start()

    def have_hidden(u):
        hid_core(u).wait_recv()
        hid_pass(u).wait_recv()

    def make_hidden(k):
        in_copy(k, gate, gate_v, ld_g).wait()
        in_copy(k, up, up_v, ld_u).wait()
        f = ds(k * FC, FC, FC)

        def rows(i, carry):
            r = ds(i * STEP, STEP, STEP)
            g = gate_v[r, f].astype(F32)
            u = up_v[r, f].astype(F32)
            hid[ds(c * HALF + i * STEP, STEP, STEP), f] = (g * sigmoid(g) * u).astype(BF16)
            return carry

        lax.fori_loop(0, HALF // STEP, rows, 0)
        for u in (2 * k, 2 * k + 1):
            hid_pair(u).start()
            hid_core(u).start()

    def dot(rows, u):
        return jnp.dot(rows, hid[:, ds(u * HF, HF, HF)], preferred_element_type=F32)

    def unit_z(k):
        return jnp.maximum(k, 2 * k - 3)

    def unit_y(k):
        return 2 * k + 4

    def of_layer(j):
        return g_t[2 * BLK * j : 2 * BLK * (j + 1), :]

    def of_column(s, h):
        return jnp.concatenate(
            [g_t[(4 * h + s) * BLK : (4 * h + s + 1) * BLK, :], g_t[(4 * h + 2 + s) * BLK : (4 * h + 3 + s) * BLK, :]], 0
        )

    def z0(k, half):
        return send(zs0.at[k, half], zr0.at[k, half], z0_s.at[k, half], z0_r.at[k, half], (below, above)[half])

    def z1(k, way):
        return send(zs1.at[k, way], zr1.at[k, way], z1_s.at[k, way], z1_r.at[k, way], (above, below)[way])

    def z_last(k):
        return send(es.at[k], er.at[k], e_s.at[k], e_r.at[k], across)

    def y_first(k):
        return send(as_.at[k], ar.at[k], a_s.at[k], a_r.at[k], across)

    def y0(k, half):
        return send(ys0.at[k, half], yr0.at[k, half], y0_s.at[k, half], y0_r.at[k, half], (below, above)[half])

    def y1(k, way):
        return send(ys1.at[k, way], yr1.at[k, way], y1_s.at[k, way], y1_r.at[k, way], (above, below)[way])

    def z_stage0(k):
        part = dot(of_layer(0), unit_z(k)).astype(BF16)
        for half in (0, 1):
            zs0[k, half] = part[:, half * BLK : (half + 1) * BLK]
            z0(k, half).start()

    def y_stage0(k):
        for h in (0, 1):
            as_[k, 2 * BLK * h : 2 * BLK * (h + 1), :] = dot(of_column(1, h), unit_y(k)).astype(BF16)
        y_first(k).start()

    def z_stage1(k):
        for way in (0, 1):
            part = dot(of_layer(1 + way), unit_z(k))
            half = 1 - way
            z0(k, half).wait_recv()
            lo, hi = part[:, :BLK], part[:, BLK:]
            got = zr0[k, half].astype(F32)
            if half:
                hi = hi + got
            else:
                lo = lo + got
            zs1[k, way, :, :BLK] = lo.astype(BF16)
            zs1[k, way, :, BLK:] = hi.astype(BF16)
            z1(k, way).start()

    def y_stage1(k):
        parts = [dot(of_column(0, h), unit_y(k)) for h in (0, 1)]
        y_first(k).wait_recv()
        first = parts[0] + ar[k, : 2 * BLK, :].astype(F32)
        far = first[:BLK, :].astype(BF16)
        for half in (0, 1):
            ys0[k, half] = far[:, half * BLK : (half + 1) * BLK]
            y0(k, half).start()
        ykeep[k, :BLK, :] = first[BLK:, :]
        ykeep[k, BLK:, :] = parts[1] + ar[k, 2 * BLK :, :].astype(F32)

    def z_stage2(k):
        part = dot(of_layer(3), unit_z(k))
        for way in (0, 1):
            z1(k, way).wait_recv()
            part = part + zr1[k, way].astype(F32)
        es[k] = part[BLK:, :].astype(BF16)
        z_last(k).start()
        zkeep[k] = part[:BLK, :]

    def y_stage2(k):
        for way in (0, 1):
            half = 1 - way
            y0(k, half).wait_recv()
            got = yr0[k, half].astype(F32)
            lo, hi = ykeep[k, BLK * way : BLK * (way + 1), :BLK], ykeep[k, BLK * way : BLK * (way + 1), BLK:]
            if half:
                hi = hi + got
            else:
                lo = lo + got
            ys1[k, way, :, :BLK] = lo.astype(BF16)
            ys1[k, way, :, BLK:] = hi.astype(BF16)
            y1(k, way).start()

    def z_stage3(k):
        z_last(k).wait_recv()
        total = zkeep[k] + er[k].astype(F32)
        wout[ds(unit_z(k) * HF, HF, HF), :] = (total * SCALE).T.astype(BF16)

    def y_stage3(k):
        total = ykeep[k, 2 * BLK :, :]
        for way in (0, 1):
            y1(k, way).wait_recv()
            total = total + yr1[k, way].astype(F32)
        wout[ds(unit_y(k) * HF, HF, HF), :] = (total * SCALE).T.astype(BF16)

    def w_copy(k):
        slot = lax.rem(k, 2)
        return pltpu.make_async_copy(w.at[ds(k * FC, FC, FC)], wbuf.at[slot], ld_w.at[slot])

    def gh_send(k):
        return send(ghs.at[k, ds((1 - c) * HALF, HALF, HALF)], ghr.at[k], gh_s.at[k], gh_r.at[k], core)

    def grad_hidden(k):
        w_copy(k).wait()

        def tile(n, carry):
            f = ds(n * HF, HF, HF)
            ghs[k, :, f] = lax.dot_general(
                g_own[...], wbuf[lax.rem(k, 2), f, :], (((1,), (1,)), ((), ())), preferred_element_type=F32
            ).astype(BF16)
            return carry

        lax.fori_loop(0, 2, tile, 0)
        gh_send(k).start()

        @pl.when(k + 2 < NC)
        def _():
            w_copy(k + 2).start()

    def grad_gate(k):
        gh_send(k).wait_recv()
        f = ds(k * FC, FC, FC)

        def rows(i, carry):
            r = ds(i * STEP, STEP, STEP)
            g = gate_v[r, f].astype(F32)
            u = up_v[r, f].astype(F32)
            grad = ghs[k, ds(c * HALF + i * STEP, STEP, STEP), :].astype(F32) + ghr[k, r, :].astype(F32)
            sig = sigmoid(g)
            gate_v[r, f] = (grad * u * (sig * (1.0 + g * (1.0 - sig)))).astype(BF16)
            up_v[r, f] = (grad * (g * sig)).astype(BF16)
            return carry

        lax.fori_loop(0, HALF // STEP, rows, 0)

    def sent(u):
        hid_core(u).wait_send()
        hid_pair(u).wait_send()
        hid_pass(u).wait_send()

    def sent_z(k):
        for i in (0, 1):
            z0(k, i).wait_send()
            z1(k, i).wait_send()
        z_last(k).wait_send()

    def sent_y(k):
        for i in (0, 1):
            y0(k, i).wait_send()
            y1(k, i).wait_send()
        y_first(k).wait_send()

    def sent_x(j):
        for s in range(4):
            for side in (0, 1):
                own_direct(block_of(j, s), side).wait_send()
                own_forward(block_of(j, s), side).wait_send()
        for s in (0, 1):
            pair_send(j, s).wait_send()
        for side in (0, 1):
            pair_direct(j, side).wait_send()
            pair_forward(j, side).wait_send()

    def loop(lo, hi, step):
        def run(i, carry):
            step(i)
            return carry

        lax.fori_loop(lo, hi, run, 0)

    def load(k):
        in_copy(k, gate, gate_v, ld_g).start()
        in_copy(k, up, up_v, ld_u).start()

    def pair_start(j):
        for s in (0, 1):
            pair_send(j, s).start()

    loop(0, NC, load)
    own_copy().start()
    w_copy(0).start()
    w_copy(1).start()
    pl.semaphore_wait(barrier, 7)
    own_start(0, 0)
    pair_start(0)
    own_start(1, 0)
    pair_start(1)

    make_hidden(0)
    pair_start(2)
    pair_start(3)
    own_copy().wait()

    def turn(j):
        own_end(j, 0)
        for side in (0, 1):
            pair_forward(j, side).wait_recv()
        for s in (0, 1):
            rows = ds((j * 2 + s) * BLK, BLK, BLK)
            g_t[rows, :TOK] = g_own[:, cols(block_of(j, s))].T
            g_t[rows, TOK:] = g_pair[:, cols(j * 2 + s)].T

    def gather(t):
        make_hidden(t + 1)

        @pl.when(jnp.logical_and(t >= 3, t < 5))
        def _():
            have_hidden(t - 3)
            z_stage0(t - 3)

        @pl.when(t >= 2)
        def _():
            turn(t - 2)

        @pl.when(t == 4)
        def _():
            loop(0, 2, z_stage1)

        @pl.when(jnp.logical_and(t >= 1, t < 5))
        def _():
            for side in (0, 1):
                pair_direct(t - 1, side).wait_recv()
                pair_forward(t - 1, side).start()

        @pl.when(t == 4)
        def _():
            loop(0, 4, lambda j: own_start(j, 2))

        @pl.when(t < 4)
        def _():
            for s in (0, 1):
                pair_send(t, s).wait_recv()
            for side in (0, 1):
                pair_direct(t, side).start()

        @pl.when(jnp.logical_and(t >= 1, t < 3))
        def _():
            pass_on(t - 1)

        @pl.when(t < 2)
        def _():
            own_start(t + 2, 0)

        @pl.when(t < 4)
        def _():
            own_pass(t, 0)

    loop(0, NC - 1, gather)

    def products(k, on):
        @pl.when(on)
        def _():
            grad_hidden(k)

    def gates(k, on):
        @pl.when(on)
        def _():
            grad_gate(k)

    def body(i):
        @pl.when(i < NC)
        def _():
            pass_on(2 * i)
            pass_on(2 * i + 1)

        @pl.when(i == 2)
        def _():
            loop(0, 4, lambda j: own_pass(j, 2))

        @pl.when(i == 3)
        def _():
            loop(0, 4, lambda j: own_end(j, 2))

        def early(d):
            products(jnp.where(i < 5, 2 * i - 6, i - 1) + d, jnp.logical_and(i >= 3, i < jnp.where(d == 0, 8, 5)))

        loop(0, 2, early)

        @pl.when(i < NC)
        def _():
            have_hidden(2 * i + 1)
            z_stage0(i + 2)
            have_hidden(2 * i)

            @pl.when(i == 1)
            def _():
                z_stage0(2)

            @pl.when(i >= 2)
            def _():
                y_stage0(i - 2)

        @pl.when(jnp.logical_and(i >= 2, i < NC + 1))
        def _():
            loop(jnp.where(i == 2, 2, i + 1), i + 2, z_stage1)

        @pl.when(jnp.logical_and(i != 2, i < NC + 2))
        def _():
            loop(jnp.where(i == 1, 0, jnp.where(i == 3, 2, i)), i + 1, z_stage2)

        @pl.when(jnp.logical_and(i >= 3, i < NY + 3))
        def _():
            y_stage1(i - 3)

        @pl.when(jnp.logical_and(i >= 4, i < NY + 4))
        def _():
            y_stage2(i - 4)

        def late(d):
            gates(jnp.where(i < 6, 2 * i - 8, i - 2) + d, jnp.logical_and(i >= 4, i < jnp.where(d == 0, 9, 6)))

        loop(0, 2, late)

        @pl.when(jnp.logical_and(i >= 2, i != 3))
        def _():
            loop(jnp.where(i == 2, 0, jnp.where(i == 4, 2, i - 1)), i, z_stage3)

        @pl.when(i >= 5)
        def _():
            y_stage3(i - 5)

        @pl.when(i == NC + 1)
        def _():
            loop(0, NU, sent)
            loop(0, NC, lambda k: gh_send(k).wait_send())
            loop(0, 4, sent_x)

    loop(1, NC + 3, body)

    loop(0, NZ, sent_z)
    loop(0, NY, sent_y)


def on_device(grad_out, gate_pre, up_pre, down_weight):
    dma = pltpu.SemaphoreType.DMA
    vmem = lambda *shape: pltpu.VMEM(shape, BF16)
    scratch = [
        vmem(TOK, DM), vmem(TOK, 8 * BLK), vmem(8 * BLK, 2 * TOK), vmem(2 * TOK, FF),
        vmem(2, FC, DM), vmem(NC, TOK, FC), vmem(NC, HALF, FC),
        vmem(NZ, 2, 2 * BLK, BLK), vmem(NZ, 2, 2 * BLK, BLK), vmem(NZ, 2, 2 * BLK, HF), vmem(NZ, 2, 2 * BLK, HF),
        vmem(NZ, BLK, HF), vmem(NZ, BLK, HF), pltpu.VMEM((NZ, BLK, HF), F32),
        vmem(NY, 4 * BLK, HF), vmem(NY, 4 * BLK, HF), vmem(NY, 2, BLK, BLK), vmem(NY, 2, BLK, BLK),
        vmem(NY, 2, BLK, HF), vmem(NY, 2, BLK, HF), pltpu.VMEM((NY, 3 * BLK, HF), F32),
        dma((16, 2)), dma((16, 2)), dma((16, 2)), dma((16, 2)), dma((8,)), dma((8,)),
        dma((4, 2)), dma((4, 2)), dma((4, 2)), dma((4, 2)),
        dma((NU,)), dma((NU,)), dma((NU,)), dma((NU,)), dma((NU,)), dma((NU,)),
        dma((NZ, 2)), dma((NZ, 2)), dma((NZ, 2)), dma((NZ, 2)), dma((NZ,)), dma((NZ,)),
        dma((NY,)), dma((NY,)), dma((NY, 2)), dma((NY, 2)), dma((NY, 2)), dma((NY, 2)),
        dma((NC,)), dma((NC,)), dma((NC,)), dma((NC,)), dma, dma((2,)),
    ]
    anywhere = pl.BlockSpec(memory_space=pl.ANY)
    grad_gate, grad_up, grad_weight = pl.pallas_call(
        kernel,
        out_shape=(pltpu.VMEM((HALF, FF), BF16), pltpu.VMEM((HALF, FF), BF16), pltpu.VMEM((FF, BLK), BF16)),
        in_specs=[pl.BlockSpec(memory_space=pltpu.HBM)] + [anywhere] * 3,
        out_specs=(pl.BlockSpec(memory_space=pltpu.VMEM),) * 3,
        scratch_shapes=scratch,
        compiler_params=pltpu.CompilerParams(
            collective_id=0, has_side_effects=True, vmem_limit_bytes=48 * 2**20
        ),
        cost_estimate=pl.CostEstimate(flops=4 * TOK * FF * DM, bytes_accessed=24 * 10**6, transcendentals=2 * HALF * FF),
    )(grad_out[0], gate_pre[0], up_pre[0], down_weight)
    return grad_gate[None], grad_up[None], grad_weight


def solution(mesh):
    in_specs = (
        P("depth", "row", "col"),
        P("depth", "col", "row"),
        P("depth", "col", "row"),
        P("row", "col"),
    )
    out_specs = (P("depth", "col", "row"), P("depth", "col", "row"), P("row", ("col", "depth")))
    return jax.shard_map(
        on_device, mesh=mesh, in_specs=in_specs, out_specs=out_specs, check_vma=False
    )
```

```python
import jax
import jax.numpy as jnp
from jax import lax
from jax.experimental import pallas as pl
from jax.experimental.pallas import tpu as pltpu
from jax.sharding import PartitionSpec as P

MESH = pl.DeviceIdType.MESH
BF16, F32 = jnp.bfloat16, jnp.float32

TOK, FF, DM = 512, 3584, 2048
HALF = TOK // 2
ROWS = TOK // 4
FC = 512
NC = FF // FC
HF = FC // 2
NU = FF // HF
NY = 5
NZ = NU - NY
BLK = 128
STEP = 32
SCALE = float(16 * TOK) ** -0.5


def sigmoid(v):
    return 0.5 * jnp.tanh(0.5 * v) + 0.5


def kernel(
    go, gate, up, w, gate_v, up_v, wout,
    g_own, g_pair, g_t, hid, wbuf, ghs, ghr,
    zs0, zr0, zs1, zr1, es, er, zkeep,
    as_, ar, ys0, yr0, ys1, yr1, ykeep,
    xo_s, xo_r, xf_s, xf_r, pp_s, pp_r, px_s, px_r, pf_s, pf_r,
    hc_s, hc_r, hp_s, hp_r, hf_s, hf_r,
    z0_s, z0_r, z1_s, z1_r, e_s, e_r, a_s, a_r, y0_s, y0_r, y1_s, y1_r,
    gh_s, gh_r, ld_g, ld_u, ld_o, ld_w,
):
    x, c, q = lax.axis_index("row"), lax.axis_index("col"), lax.axis_index("depth")
    z, y = lax.div(q, 4), lax.rem(q, 4)
    odd = lax.rem(y, 2)
    y_pair = y + 1 - 2 * odd
    y_sum = lax.rem(y + 3 + 2 * odd, 4)
    y_pair_sum = lax.rem(y_pair + 3 + 2 * (1 - odd), 4)
    core = (x, 1 - c, q)
    right, left = (lax.rem(x + 1, 4), c, q), (lax.rem(x + 3, 4), c, q)
    sides = (right, left)
    pair = (x, c, z * 4 + y_pair)
    across = (x, c, z * 4 + y_sum)
    above, below = (x, c, lax.rem(z + 1, 4) * 4 + y), (x, c, lax.rem(z + 3, 4) * 4 + y)

    barrier = pltpu.get_barrier_semaphore()
    for other in (core, right, left, pair, across, above, below):
        pl.semaphore_signal(barrier, inc=1, device_id=other, device_id_type=MESH)
    def send(src, dst, ss, rs, device):
        return pltpu.make_async_remote_copy(
            src_ref=src, dst_ref=dst, send_sem=ss, recv_sem=rs, device_id=device, device_id_type=MESH
        )

    def ds(start, size, unit):
        return pl.ds(pl.multiple_of(start, unit), size)

    def layer(j):
        return lax.rem(z + jnp.where(j == 0, 2, jnp.where(j == 1, 1, jnp.where(j == 2, 3, 0))), 4)

    def block_of(j, s):
        column = (y, y_sum, y_pair, y_pair_sum)[s]
        return layer(j) * 4 + column

    def cols(b):
        return ds(b * BLK, BLK, BLK)

    def own_copy():
        return pltpu.make_async_copy(go, g_own.at[ds(x * ROWS, ROWS, ROWS)], ld_o)

    def own_direct(b, side):
        return send(
            go.at[:, cols(b)], g_own.at[ds(x * ROWS, ROWS, ROWS), cols(b)],
            xo_s.at[b, side], xo_r.at[b, side], sides[side],
        )

    def own_forward(b, side):
        source = lax.rem(x + (3 if side == 0 else 1), 4)
        rows = ds(source * ROWS + side * (ROWS // 2), ROWS // 2, ROWS // 2)
        return send(
            g_own.at[rows, cols(b)], g_own.at[rows, cols(b)], xf_s.at[b, side], xf_r.at[b, side], sides[side]
        )

    def pair_send(j, s):
        i = j * 2 + s
        return send(
            go.at[:, cols(block_of(j, s + 2))], g_pair.at[ds(x * ROWS, ROWS, ROWS), cols(i)],
            pp_s.at[i], pp_r.at[i], pair,
        )

    def pair_cols(j):
        return ds(j * 2 * BLK, 2 * BLK, 2 * BLK)

    def pair_direct(j, side):
        view = g_pair.at[ds(x * ROWS, ROWS, ROWS), pair_cols(j)]
        return send(view, view, px_s.at[j, side], px_r.at[j, side], sides[side])

    def pair_forward(j, side):
        source = lax.rem(x + (3 if side == 0 else 1), 4)
        view = g_pair.at[ds(source * ROWS + side * (ROWS // 2), ROWS // 2, ROWS // 2), pair_cols(j)]
        return send(view, view, pf_s.at[j, side], pf_r.at[j, side], sides[side])

    def own_start(j, first):
        for s in (first, first + 1):
            for side in (0, 1):
                own_direct(block_of(j, s), side).start()

    def own_pass(j, first):
        for s in (first, first + 1):
            b = block_of(j, s)
            for side in (0, 1):
                own_direct(b, side).wait_recv()
                own_forward(b, side).start()

    def own_end(j, first):
        for s in (first, first + 1):
            for side in (0, 1):
                own_forward(block_of(j, s), side).wait_recv()

    def in_copy(k, src, dst, sem):
        f = ds(k * FC, FC, FC)
        return pltpu.make_async_copy(src.at[:, f], dst.at[:, f], sem.at[k])

    def hid_view(group, u):
        return hid.at[ds(group * TOK + c * HALF, HALF, HALF), ds(u * HF, HF, HF)]

    def hid_core(u):
        return send(hid_view(0, u), hid_view(0, u), hc_s.at[u], hc_r.at[u], core)

    def hid_pair(u):
        return send(hid_view(0, u), hid_view(1, u), hp_s.at[u], hp_r.at[u], pair)

    def hid_pass(u):
        return send(hid_view(1, u), hid_view(1, u), hf_s.at[u], hf_r.at[u], core)

    def pass_on(u):
        hid_pair(u).wait_recv()
        hid_pass(u).start()

    def have_hidden(u):
        hid_core(u).wait_recv()
        hid_pass(u).wait_recv()

    def make_hidden(k):
        in_copy(k, gate, gate_v, ld_g).wait()
        in_copy(k, up, up_v, ld_u).wait()
        f = ds(k * FC, FC, FC)

        def rows(i, carry):
            r = ds(i * STEP, STEP, STEP)
            g = gate_v[r, f].astype(F32)
            u = up_v[r, f].astype(F32)
            hid[ds(c * HALF + i * STEP, STEP, STEP), f] = (g * sigmoid(g) * u).astype(BF16)
            return carry

        lax.fori_loop(0, HALF // STEP, rows, 0)
        for u in (2 * k, 2 * k + 1):
            hid_pair(u).start()
            hid_core(u).start()

    def dot(rows, u):
        return jnp.dot(rows, hid[:, ds(u * HF, HF, HF)], preferred_element_type=F32)

    def unit_z(k):
        return jnp.maximum(k, 2 * k - 3)

    def unit_y(k):
        return 2 * k + 4

    def of_layer(j):
        return g_t[2 * BLK * j : 2 * BLK * (j + 1), :]

    def of_column(s, h):
        return jnp.concatenate(
            [g_t[(4 * h + s) * BLK : (4 * h + s + 1) * BLK, :], g_t[(4 * h + 2 + s) * BLK : (4 * h + 3 + s) * BLK, :]], 0
        )

    def z0(k, half):
        return send(zs0.at[k, half], zr0.at[k, half], z0_s.at[k, half], z0_r.at[k, half], (below, above)[half])

    def z1(k, way):
        return send(zs1.at[k, way], zr1.at[k, way], z1_s.at[k, way], z1_r.at[k, way], (above, below)[way])

    def z_last(k):
        return send(es.at[k], er.at[k], e_s.at[k], e_r.at[k], across)

    def y_first(k):
        return send(as_.at[k], ar.at[k], a_s.at[k], a_r.at[k], across)

    def y0(k, half):
        return send(ys0.at[k, half], yr0.at[k, half], y0_s.at[k, half], y0_r.at[k, half], (below, above)[half])

    def y1(k, way):
        return send(ys1.at[k, way], yr1.at[k, way], y1_s.at[k, way], y1_r.at[k, way], (above, below)[way])

    def z_stage0(k):
        part = dot(of_layer(0), unit_z(k)).astype(BF16)
        for half in (0, 1):
            zs0[k, half] = part[:, half * BLK : (half + 1) * BLK]
            z0(k, half).start()

    def y_stage0(k):
        for h in (0, 1):
            as_[k, 2 * BLK * h : 2 * BLK * (h + 1), :] = dot(of_column(1, h), unit_y(k)).astype(BF16)
        y_first(k).start()

    def z_stage1(k):
        for way in (0, 1):
            part = dot(of_layer(1 + way), unit_z(k))
            half = 1 - way
            z0(k, half).wait_recv()
            lo, hi = part[:, :BLK], part[:, BLK:]
            got = zr0[k, half].astype(F32)
            if half:
                hi = hi + got
            else:
                lo = lo + got
            zs1[k, way, :, :BLK] = lo.astype(BF16)
            zs1[k, way, :, BLK:] = hi.astype(BF16)
            z1(k, way).start()

    def y_stage1(k):
        parts = [dot(of_column(0, h), unit_y(k)) for h in (0, 1)]
        y_first(k).wait_recv()
        first = parts[0] + ar[k, : 2 * BLK, :].astype(F32)
        far = first[:BLK, :].astype(BF16)
        for half in (0, 1):
            ys0[k, half] = far[:, half * BLK : (half + 1) * BLK]
            y0(k, half).start()
        ykeep[k, :BLK, :] = first[BLK:, :]
        ykeep[k, BLK:, :] = parts[1] + ar[k, 2 * BLK :, :].astype(F32)

    def z_stage2(k):
        part = dot(of_layer(3), unit_z(k))
        for way in (0, 1):
            z1(k, way).wait_recv()
            part = part + zr1[k, way].astype(F32)
        es[k] = part[BLK:, :].astype(BF16)
        z_last(k).start()
        zkeep[k] = part[:BLK, :]

    def y_stage2(k):
        for way in (0, 1):
            half = 1 - way
            y0(k, half).wait_recv()
            got = yr0[k, half].astype(F32)
            lo, hi = ykeep[k, BLK * way : BLK * (way + 1), :BLK], ykeep[k, BLK * way : BLK * (way + 1), BLK:]
            if half:
                hi = hi + got
            else:
                lo = lo + got
            ys1[k, way, :, :BLK] = lo.astype(BF16)
            ys1[k, way, :, BLK:] = hi.astype(BF16)
            y1(k, way).start()

    def z_stage3(k):
        z_last(k).wait_recv()
        total = zkeep[k] + er[k].astype(F32)
        wout[ds(unit_z(k) * HF, HF, HF), :] = (total * SCALE).T.astype(BF16)

    def y_stage3(k):
        total = ykeep[k, 2 * BLK :, :]
        for way in (0, 1):
            y1(k, way).wait_recv()
            total = total + yr1[k, way].astype(F32)
        wout[ds(unit_y(k) * HF, HF, HF), :] = (total * SCALE).T.astype(BF16)

    def w_copy(k):
        slot = lax.rem(k, 2)
        return pltpu.make_async_copy(w.at[ds(k * FC, FC, FC)], wbuf.at[slot], ld_w.at[slot])

    def gh_send(k):
        return send(ghs.at[k, ds((1 - c) * HALF, HALF, HALF)], ghr.at[k], gh_s.at[k], gh_r.at[k], core)

    def grad_hidden(k):
        w_copy(k).wait()

        def tile(n, carry):
            f = ds(n * HF, HF, HF)
            ghs[k, :, f] = lax.dot_general(
                g_own[...], wbuf[lax.rem(k, 2), f, :], (((1,), (1,)), ((), ())), preferred_element_type=F32
            ).astype(BF16)
            return carry

        lax.fori_loop(0, 2, tile, 0)
        gh_send(k).start()

        @pl.when(k + 2 < NC)
        def _():
            w_copy(k + 2).start()

    def grad_gate(k):
        gh_send(k).wait_recv()
        f = ds(k * FC, FC, FC)

        def rows(i, carry):
            r = ds(i * STEP, STEP, STEP)
            g = gate_v[r, f].astype(F32)
            u = up_v[r, f].astype(F32)
            grad = ghs[k, ds(c * HALF + i * STEP, STEP, STEP), :].astype(F32) + ghr[k, r, :].astype(F32)
            sig = sigmoid(g)
            gate_v[r, f] = (grad * u * (sig * (1.0 + g * (1.0 - sig)))).astype(BF16)
            up_v[r, f] = (grad * (g * sig)).astype(BF16)
            return carry

        lax.fori_loop(0, HALF // STEP, rows, 0)

    def sent(u):
        hid_core(u).wait_send()
        hid_pair(u).wait_send()
        hid_pass(u).wait_send()

    def sent_z(k):
        for i in (0, 1):
            z0(k, i).wait_send()
            z1(k, i).wait_send()
        z_last(k).wait_send()

    def sent_y(k):
        for i in (0, 1):
            y0(k, i).wait_send()
            y1(k, i).wait_send()
        y_first(k).wait_send()

    def sent_x(j):
        for s in range(4):
            for side in (0, 1):
                own_direct(block_of(j, s), side).wait_send()
                own_forward(block_of(j, s), side).wait_send()
        for s in (0, 1):
            pair_send(j, s).wait_send()
        for side in (0, 1):
            pair_direct(j, side).wait_send()
            pair_forward(j, side).wait_send()

    def loop(lo, hi, step):
        def run(i, carry):
            step(i)
            return carry

        lax.fori_loop(lo, hi, run, 0)

    def load(k):
        in_copy(k, gate, gate_v, ld_g).start()
        in_copy(k, up, up_v, ld_u).start()

    def pair_start(j):
        for s in (0, 1):
            pair_send(j, s).start()

    loop(0, NC, load)
    own_copy().start()
    w_copy(0).start()
    w_copy(1).start()
    pl.semaphore_wait(barrier, 7)
    own_start(0, 0)
    pair_start(0)
    own_start(1, 0)
    pair_start(1)

    make_hidden(0)
    pair_start(2)
    pair_start(3)
    loop(1, 5, make_hidden)
    own_copy().wait()

    def turn(j):
        own_end(j, 0)
        for side in (0, 1):
            pair_forward(j, side).wait_recv()
        for s in (0, 1):
            rows = ds((j * 2 + s) * BLK, BLK, BLK)
            g_t[rows, :TOK] = g_own[:, cols(block_of(j, s))].T
            g_t[rows, TOK:] = g_pair[:, cols(j * 2 + s)].T

    def gather(t):
        @pl.when(jnp.logical_and(t >= 2, t < 4))
        def _():
            pass_on(t - 2)

        @pl.when(t >= 2)
        def _():
            turn(t - 2)

        @pl.when(t == 4)
        def _():
            loop(0, 2, z_stage1)

        @pl.when(jnp.logical_and(t >= 1, t < 5))
        def _():
            for side in (0, 1):
                pair_direct(t - 1, side).wait_recv()
                pair_forward(t - 1, side).start()

        @pl.when(t == 4)
        def _():
            loop(0, 4, lambda j: own_start(j, 2))

        @pl.when(t < 4)
        def _():
            for s in (0, 1):
                pair_send(t, s).wait_recv()
            for side in (0, 1):
                pair_direct(t, side).start()

        @pl.when(t < 2)
        def _():
            own_start(t + 2, 0)

        @pl.when(t < 4)
        def _():
            own_pass(t, 0)

        @pl.when(jnp.logical_and(t >= 2, t < 4))
        def _():
            have_hidden(t - 2)
            z_stage0(t - 2)

        @pl.when(t + 5 < NC)
        def _():
            make_hidden(t + 5)

    loop(0, 6, gather)

    def products(k, on):
        @pl.when(on)
        def _():
            grad_hidden(k)

    def gates(k, on):
        @pl.when(on)
        def _():
            grad_gate(k)

    def body(i):
        @pl.when(i < NC)
        def _():
            pass_on(2 * i)
            pass_on(2 * i + 1)

        @pl.when(i == 2)
        def _():
            loop(0, 4, lambda j: own_pass(j, 2))

        @pl.when(i == 3)
        def _():
            loop(0, 4, lambda j: own_end(j, 2))

        products(2 * i - 6, jnp.logical_and(i >= 3, i < 7))
        gates(2 * i - 8, jnp.logical_and(i >= 4, i < 8))

        @pl.when(i < NC)
        def _():
            have_hidden(2 * i)

            @pl.when(i == 1)
            def _():
                z_stage0(2)

            @pl.when(i >= 2)
            def _():
                y_stage0(i - 2)

            have_hidden(2 * i + 1)
            z_stage0(i + 2)

        @pl.when(jnp.logical_and(i >= 2, i < NC + 1))
        def _():
            loop(jnp.where(i == 2, 2, i + 1), i + 2, z_stage1)

        products(2 * i - 5, jnp.logical_and(i >= 3, i < 6))

        @pl.when(jnp.logical_and(i >= 3, i < NY + 3))
        def _():
            y_stage1(i - 3)

        @pl.when(jnp.logical_and(i != 2, i < NC + 2))
        def _():
            loop(jnp.where(i == 1, 0, jnp.where(i == 3, 2, i)), i + 1, z_stage2)

        @pl.when(jnp.logical_and(i >= 4, i < NY + 4))
        def _():
            y_stage2(i - 4)

        @pl.when(jnp.logical_and(i >= 2, i != 3))
        def _():
            loop(jnp.where(i == 2, 0, jnp.where(i == 4, 2, i - 1)), i, z_stage3)

        gates(2 * i - 7, jnp.logical_and(i >= 4, i < 7))

        @pl.when(i >= 5)
        def _():
            y_stage3(i - 5)

        @pl.when(i == NC + 1)
        def _():
            loop(0, NU, sent)
            loop(0, NC, lambda k: gh_send(k).wait_send())
            loop(0, 4, sent_x)

    loop(1, NC + 3, body)

    loop(0, NZ, sent_z)
    loop(0, NY, sent_y)


def write_out(gate_v, up_v, weight_v, o_gate, o_up, o_weight, sems):
    copies = []
    for src, dst in ((gate_v, o_gate), (up_v, o_up), (weight_v, o_weight)):
        rows = src.shape[0] // 2
        for part in (0, 1):
            r = pl.ds(part * rows, rows)
            copies.append(pltpu.make_async_copy(src.at[r], dst.at[r], sems.at[len(copies)]))
    for copy in copies:
        copy.start()
    for copy in copies:
        copy.wait()


def on_device(grad_out, gate_pre, up_pre, down_weight):
    dma = pltpu.SemaphoreType.DMA
    vmem = lambda *shape: pltpu.VMEM(shape, BF16)
    scratch = [
        vmem(TOK, DM), vmem(TOK, 8 * BLK), vmem(8 * BLK, 2 * TOK), vmem(2 * TOK, FF),
        vmem(2, FC, DM), vmem(NC, TOK, FC), vmem(NC, HALF, FC),
        vmem(NZ, 2, 2 * BLK, BLK), vmem(NZ, 2, 2 * BLK, BLK), vmem(NZ, 2, 2 * BLK, HF), vmem(NZ, 2, 2 * BLK, HF),
        vmem(NZ, BLK, HF), vmem(NZ, BLK, HF), pltpu.VMEM((NZ, BLK, HF), F32),
        vmem(NY, 4 * BLK, HF), vmem(NY, 4 * BLK, HF), vmem(NY, 2, BLK, BLK), vmem(NY, 2, BLK, BLK),
        vmem(NY, 2, BLK, HF), vmem(NY, 2, BLK, HF), pltpu.VMEM((NY, 3 * BLK, HF), F32),
        dma((16, 2)), dma((16, 2)), dma((16, 2)), dma((16, 2)), dma((8,)), dma((8,)),
        dma((4, 2)), dma((4, 2)), dma((4, 2)), dma((4, 2)),
        dma((NU,)), dma((NU,)), dma((NU,)), dma((NU,)), dma((NU,)), dma((NU,)),
        dma((NZ, 2)), dma((NZ, 2)), dma((NZ, 2)), dma((NZ, 2)), dma((NZ,)), dma((NZ,)),
        dma((NY,)), dma((NY,)), dma((NY, 2)), dma((NY, 2)), dma((NY, 2)), dma((NY, 2)),
        dma((NC,)), dma((NC,)), dma((NC,)), dma((NC,)), dma, dma((2,)),
    ]
    anywhere = pl.BlockSpec(memory_space=pl.ANY)
    results = pl.pallas_call(
        kernel,
        out_shape=(pltpu.VMEM((HALF, FF), BF16), pltpu.VMEM((HALF, FF), BF16), pltpu.VMEM((FF, BLK), BF16)),
        in_specs=[pl.BlockSpec(memory_space=pltpu.HBM)] + [anywhere] * 3,
        out_specs=(pl.BlockSpec(memory_space=pltpu.VMEM),) * 3,
        scratch_shapes=scratch,
        compiler_params=pltpu.CompilerParams(
            collective_id=0, has_side_effects=True, vmem_limit_bytes=48 * 2**20
        ),
        cost_estimate=pl.CostEstimate(flops=4 * TOK * FF * DM, bytes_accessed=24 * 10**6, transcendentals=2 * HALF * FF),
    )(pltpu.with_memory_space_constraint(grad_out[0], pltpu.HBM), gate_pre[0], up_pre[0], down_weight)
    grad_gate, grad_up, grad_weight = pl.pallas_call(
        write_out,
        out_shape=tuple(jax.ShapeDtypeStruct(r.shape, r.dtype) for r in results),
        in_specs=[pl.BlockSpec(memory_space=pltpu.VMEM)] * 3,
        out_specs=(anywhere,) * 3,
        scratch_shapes=[dma((6,))],
        compiler_params=pltpu.CompilerParams(vmem_limit_bytes=2**20),
    )(*(pltpu.with_memory_space_constraint(r, pltpu.VMEM) for r in results))
    return grad_gate[None], grad_up[None], grad_weight


def solution(mesh):
    in_specs = (
        P("depth", "row", "col"),
        P("depth", "col", "row"),
        P("depth", "col", "row"),
        P("row", "col"),
    )
    out_specs = (P("depth", "col", "row"), P("depth", "col", "row"), P("row", ("col", "depth")))
    return jax.shard_map(
        on_device, mesh=mesh, in_specs=in_specs, out_specs=out_specs, check_vma=False
    )
```

```python
import jax
import jax.numpy as jnp
from jax import lax
from jax.experimental import pallas as pl
from jax.experimental.pallas import tpu as pltpu
from jax.sharding import PartitionSpec as P

MESH = pl.DeviceIdType.MESH
BF16, F32 = jnp.bfloat16, jnp.float32

TOK, FF, DM = 512, 3584, 2048
HALF = TOK // 2
ROWS = TOK // 4
FC = 512
NC = FF // FC
HF = FC // 2
NU = FF // HF
NY = 5
NZ = NU - NY
BLK = 128
STEP = 32
SCALE = float(16 * TOK) ** -0.5


def sigmoid(v):
    return 0.5 * jnp.tanh(0.5 * v) + 0.5


def kernel(
    go, gate, up, w, gate_v, up_v, wout,
    g_own, g_pair, g_t, hid, wbuf, ghs, ghr,
    zs0, zr0, zs1, zr1, es, er, zkeep,
    as_, ar, ys0, yr0, ys1, yr1, ykeep,
    xo_s, xo_r, xf_s, xf_r, pp_s, pp_r, px_s, px_r, pf_s, pf_r,
    hc_s, hc_r, hp_s, hp_r, hf_s, hf_r,
    z0_s, z0_r, z1_s, z1_r, e_s, e_r, a_s, a_r, y0_s, y0_r, y1_s, y1_r,
    gh_s, gh_r, ld_g, ld_u, ld_o, ld_w,
):
    x, c, q = lax.axis_index("row"), lax.axis_index("col"), lax.axis_index("depth")
    z, y = lax.div(q, 4), lax.rem(q, 4)
    odd = lax.rem(y, 2)
    y_pair = y + 1 - 2 * odd
    y_sum = lax.rem(y + 3 + 2 * odd, 4)
    y_pair_sum = lax.rem(y_pair + 3 + 2 * (1 - odd), 4)
    core = (x, 1 - c, q)
    right, left = (lax.rem(x + 1, 4), c, q), (lax.rem(x + 3, 4), c, q)
    sides = (right, left)
    pair = (x, c, z * 4 + y_pair)
    across = (x, c, z * 4 + y_sum)
    above, below = (x, c, lax.rem(z + 1, 4) * 4 + y), (x, c, lax.rem(z + 3, 4) * 4 + y)

    barrier = pltpu.get_barrier_semaphore()
    for other in (core, right, left, pair, across, above, below):
        pl.semaphore_signal(barrier, inc=1, device_id=other, device_id_type=MESH)
    def send(src, dst, ss, rs, device):
        return pltpu.make_async_remote_copy(
            src_ref=src, dst_ref=dst, send_sem=ss, recv_sem=rs, device_id=device, device_id_type=MESH
        )

    def ds(start, size, unit):
        return pl.ds(pl.multiple_of(start, unit), size)

    def layer(j):
        return lax.rem(z + jnp.where(j == 0, 2, jnp.where(j == 1, 1, jnp.where(j == 2, 3, 0))), 4)

    def block_of(j, s):
        column = (y, y_sum, y_pair, y_pair_sum)[s]
        return layer(j) * 4 + column

    def cols(b):
        return ds(b * BLK, BLK, BLK)

    def own_copy():
        return pltpu.make_async_copy(go, g_own.at[ds(x * ROWS, ROWS, ROWS)], ld_o)

    def own_direct(b, side):
        return send(
            go.at[:, cols(b)], g_own.at[ds(x * ROWS, ROWS, ROWS), cols(b)],
            xo_s.at[b, side], xo_r.at[b, side], sides[side],
        )

    def own_forward(b, side):
        source = lax.rem(x + (3 if side == 0 else 1), 4)
        rows = ds(source * ROWS + side * (ROWS // 2), ROWS // 2, ROWS // 2)
        return send(
            g_own.at[rows, cols(b)], g_own.at[rows, cols(b)], xf_s.at[b, side], xf_r.at[b, side], sides[side]
        )

    def pair_send(j, s):
        i = j * 2 + s
        return send(
            go.at[:, cols(block_of(j, s + 2))], g_pair.at[ds(x * ROWS, ROWS, ROWS), cols(i)],
            pp_s.at[i], pp_r.at[i], pair,
        )

    def pair_cols(j):
        return ds(j * 2 * BLK, 2 * BLK, 2 * BLK)

    def pair_direct(j, side):
        view = g_pair.at[ds(x * ROWS, ROWS, ROWS), pair_cols(j)]
        return send(view, view, px_s.at[j, side], px_r.at[j, side], sides[side])

    def pair_forward(j, side):
        source = lax.rem(x + (3 if side == 0 else 1), 4)
        view = g_pair.at[ds(source * ROWS + side * (ROWS // 2), ROWS // 2, ROWS // 2), pair_cols(j)]
        return send(view, view, pf_s.at[j, side], pf_r.at[j, side], sides[side])

    def own_start(j, first):
        for s in (first, first + 1):
            for side in (0, 1):
                own_direct(block_of(j, s), side).start()

    def own_pass(j, first):
        for s in (first, first + 1):
            b = block_of(j, s)
            for side in (0, 1):
                own_direct(b, side).wait_recv()
                own_forward(b, side).start()

    def own_end(j, first):
        for s in (first, first + 1):
            for side in (0, 1):
                own_forward(block_of(j, s), side).wait_recv()

    def in_copy(k, src, dst, sem):
        f = ds(k * FC, FC, FC)
        return pltpu.make_async_copy(src.at[:, f], dst.at[:, f], sem.at[k])

    def hid_view(group, u):
        return hid.at[ds(group * TOK + c * HALF, HALF, HALF), ds(u * HF, HF, HF)]

    def hid_core(u):
        return send(hid_view(0, u), hid_view(0, u), hc_s.at[u], hc_r.at[u], core)

    def hid_pair(u):
        return send(hid_view(0, u), hid_view(1, u), hp_s.at[u], hp_r.at[u], pair)

    def hid_pass(u):
        return send(hid_view(1, u), hid_view(1, u), hf_s.at[u], hf_r.at[u], core)

    def pass_on(u):
        hid_pair(u).wait_recv()
        hid_pass(u).start()

    def have_hidden(u):
        hid_core(u).wait_recv()
        hid_pass(u).wait_recv()

    def make_hidden(k):
        in_copy(k, gate, gate_v, ld_g).wait()
        in_copy(k, up, up_v, ld_u).wait()
        f = ds(k * FC, FC, FC)

        def rows(i, carry):
            r = ds(i * STEP, STEP, STEP)
            g = gate_v[r, f].astype(F32)
            u = up_v[r, f].astype(F32)
            hid[ds(c * HALF + i * STEP, STEP, STEP), f] = (g * sigmoid(g) * u).astype(BF16)
            return carry

        lax.fori_loop(0, HALF // STEP, rows, 0)
        for u in (2 * k, 2 * k + 1):
            hid_pair(u).start()
            hid_core(u).start()

    def dot(rows, u):
        return jnp.dot(rows, hid[:, ds(u * HF, HF, HF)], preferred_element_type=F32)

    def unit_z(k):
        return jnp.maximum(k, 2 * k - 3)

    def unit_y(k):
        return 2 * k + 4

    def of_layer(j):
        return g_t[2 * BLK * j : 2 * BLK * (j + 1), :]

    def of_column(s, h):
        return jnp.concatenate(
            [g_t[(4 * h + s) * BLK : (4 * h + s + 1) * BLK, :], g_t[(4 * h + 2 + s) * BLK : (4 * h + 3 + s) * BLK, :]], 0
        )

    def z0(k, half):
        return send(zs0.at[k, half], zr0.at[k, half], z0_s.at[k, half], z0_r.at[k, half], (below, above)[half])

    def z1(k, way):
        return send(zs1.at[k, way], zr1.at[k, way], z1_s.at[k, way], z1_r.at[k, way], (above, below)[way])

    def z_last(k):
        return send(es.at[k], er.at[k], e_s.at[k], e_r.at[k], across)

    def y_first(k):
        return send(as_.at[k], ar.at[k], a_s.at[k], a_r.at[k], across)

    def y0(k, half):
        return send(ys0.at[k, half], yr0.at[k, half], y0_s.at[k, half], y0_r.at[k, half], (below, above)[half])

    def y1(k, way):
        return send(ys1.at[k, way], yr1.at[k, way], y1_s.at[k, way], y1_r.at[k, way], (above, below)[way])

    def z_stage0(k):
        part = dot(of_layer(0), unit_z(k)).astype(BF16)
        for half in (0, 1):
            zs0[k, half] = part[:, half * BLK : (half + 1) * BLK]
            z0(k, half).start()

    def y_stage0(k):
        for h in (0, 1):
            as_[k, 2 * BLK * h : 2 * BLK * (h + 1), :] = dot(of_column(1, h), unit_y(k)).astype(BF16)
        y_first(k).start()

    def z_stage1(k):
        for way in (0, 1):
            part = dot(of_layer(1 + way), unit_z(k))
            half = 1 - way
            z0(k, half).wait_recv()
            lo, hi = part[:, :BLK], part[:, BLK:]
            got = zr0[k, half].astype(F32)
            if half:
                hi = hi + got
            else:
                lo = lo + got
            zs1[k, way, :, :BLK] = lo.astype(BF16)
            zs1[k, way, :, BLK:] = hi.astype(BF16)
            z1(k, way).start()

    def y_stage1(k):
        parts = [dot(of_column(0, h), unit_y(k)) for h in (0, 1)]
        y_first(k).wait_recv()
        first = parts[0] + ar[k, : 2 * BLK, :].astype(F32)
        far = first[:BLK, :].astype(BF16)
        for half in (0, 1):
            ys0[k, half] = far[:, half * BLK : (half + 1) * BLK]
            y0(k, half).start()
        ykeep[k, :BLK, :] = first[BLK:, :]
        ykeep[k, BLK:, :] = parts[1] + ar[k, 2 * BLK :, :].astype(F32)

    def z_stage2(k):
        part = dot(of_layer(3), unit_z(k))
        for way in (0, 1):
            z1(k, way).wait_recv()
            part = part + zr1[k, way].astype(F32)
        es[k] = part[BLK:, :].astype(BF16)
        z_last(k).start()
        zkeep[k] = part[:BLK, :]

    def y_stage2(k):
        for way in (0, 1):
            half = 1 - way
            y0(k, half).wait_recv()
            got = yr0[k, half].astype(F32)
            lo, hi = ykeep[k, BLK * way : BLK * (way + 1), :BLK], ykeep[k, BLK * way : BLK * (way + 1), BLK:]
            if half:
                hi = hi + got
            else:
                lo = lo + got
            ys1[k, way, :, :BLK] = lo.astype(BF16)
            ys1[k, way, :, BLK:] = hi.astype(BF16)
            y1(k, way).start()

    def z_stage3(k):
        z_last(k).wait_recv()
        total = zkeep[k] + er[k].astype(F32)
        wout[ds(unit_z(k) * HF, HF, HF), :] = (total * SCALE).T.astype(BF16)

    def y_stage3(k):
        total = ykeep[k, 2 * BLK :, :]
        for way in (0, 1):
            y1(k, way).wait_recv()
            total = total + yr1[k, way].astype(F32)
        wout[ds(unit_y(k) * HF, HF, HF), :] = (total * SCALE).T.astype(BF16)

    def w_copy(k):
        slot = lax.rem(k, 2)
        return pltpu.make_async_copy(w.at[ds(k * FC, FC, FC)], wbuf.at[slot], ld_w.at[slot])

    def gh_send(k):
        return send(ghs.at[k, ds((1 - c) * HALF, HALF, HALF)], ghr.at[k], gh_s.at[k], gh_r.at[k], core)

    def grad_hidden(k):
        w_copy(k).wait()

        def tile(n, carry):
            f = ds(n * HF, HF, HF)
            ghs[k, :, f] = lax.dot_general(
                g_own[...], wbuf[lax.rem(k, 2), f, :], (((1,), (1,)), ((), ())), preferred_element_type=F32
            ).astype(BF16)
            return carry

        lax.fori_loop(0, 2, tile, 0)
        gh_send(k).start()

        @pl.when(k + 2 < NC)
        def _():
            w_copy(k + 2).start()

    def grad_gate(k):
        gh_send(k).wait_recv()
        f = ds(k * FC, FC, FC)

        def rows(i, carry):
            r = ds(i * STEP, STEP, STEP)
            g = gate_v[r, f].astype(F32)
            u = up_v[r, f].astype(F32)
            grad = ghs[k, ds(c * HALF + i * STEP, STEP, STEP), :].astype(F32) + ghr[k, r, :].astype(F32)
            sig = sigmoid(g)
            gate_v[r, f] = (grad * u * (sig * (1.0 + g * (1.0 - sig)))).astype(BF16)
            up_v[r, f] = (grad * (g * sig)).astype(BF16)
            return carry

        lax.fori_loop(0, HALF // STEP, rows, 0)

    def sent(u):
        hid_core(u).wait_send()
        hid_pair(u).wait_send()
        hid_pass(u).wait_send()

    def sent_z(k):
        for i in (0, 1):
            z0(k, i).wait_send()
            z1(k, i).wait_send()
        z_last(k).wait_send()

    def sent_y(k):
        for i in (0, 1):
            y0(k, i).wait_send()
            y1(k, i).wait_send()
        y_first(k).wait_send()

    def sent_x(j):
        for s in range(4):
            for side in (0, 1):
                own_direct(block_of(j, s), side).wait_send()
                own_forward(block_of(j, s), side).wait_send()
        for s in (0, 1):
            pair_send(j, s).wait_send()
        for side in (0, 1):
            pair_direct(j, side).wait_send()
            pair_forward(j, side).wait_send()

    def loop(lo, hi, step):
        def run(i, carry):
            step(i)
            return carry

        lax.fori_loop(lo, hi, run, 0)

    def load(k):
        in_copy(k, gate, gate_v, ld_g).start()
        in_copy(k, up, up_v, ld_u).start()

    def pair_start(j):
        for s in (0, 1):
            pair_send(j, s).start()

    loop(0, NC, load)
    own_copy().start()
    w_copy(0).start()
    w_copy(1).start()
    pl.semaphore_wait(barrier, 7)
    own_start(0, 0)
    pair_start(0)
    own_start(1, 0)
    pair_start(1)

    make_hidden(0)
    pair_start(2)
    pair_start(3)
    loop(1, 5, make_hidden)
    own_copy().wait()

    def turn(j):
        own_end(j, 0)
        for side in (0, 1):
            pair_forward(j, side).wait_recv()
        for s in (0, 1):
            rows = ds((j * 2 + s) * BLK, BLK, BLK)
            g_t[rows, :TOK] = g_own[:, cols(block_of(j, s))].T
            g_t[rows, TOK:] = g_pair[:, cols(j * 2 + s)].T

    def gather(t):
        @pl.when(jnp.logical_and(t >= 2, t < 4))
        def _():
            pass_on(t - 2)

        @pl.when(t >= 2)
        def _():
            turn(t - 2)

        @pl.when(t == 4)
        def _():
            loop(0, 2, z_stage1)

        @pl.when(jnp.logical_and(t >= 1, t < 5))
        def _():
            for side in (0, 1):
                pair_direct(t - 1, side).wait_recv()
                pair_forward(t - 1, side).start()

        @pl.when(t == 4)
        def _():
            loop(0, 4, lambda j: own_start(j, 2))

        @pl.when(t < 4)
        def _():
            for s in (0, 1):
                pair_send(t, s).wait_recv()
            for side in (0, 1):
                pair_direct(t, side).start()

        @pl.when(t < 2)
        def _():
            own_start(t + 2, 0)

        @pl.when(t < 4)
        def _():
            own_pass(t, 0)

        @pl.when(jnp.logical_and(t >= 2, t < 4))
        def _():
            have_hidden(t - 2)
            z_stage0(t - 2)

        @pl.when(t + 5 < NC)
        def _():
            make_hidden(t + 5)

    loop(0, 6, gather)

    def products(k, on):
        @pl.when(on)
        def _():
            grad_hidden(k)

    def gates(k, on):
        @pl.when(on)
        def _():
            grad_gate(k)

    def body(i):
        @pl.when(i < NC)
        def _():
            pass_on(2 * i)

        @pl.when(i == 2)
        def _():
            loop(0, 4, lambda j: own_pass(j, 2))

        @pl.when(i == 3)
        def _():
            loop(0, 4, lambda j: own_end(j, 2))

        products(jnp.where(i == 3, 0, i - 2), jnp.logical_and(i >= 3, i < NC + 2))

        @pl.when(i < NC)
        def _():
            pass_on(2 * i + 1)

        gates(0, i == 4)

        @pl.when(jnp.logical_and(i >= 4, i < NY + 4))
        def _():
            y_stage1(i - 4)

        @pl.when(jnp.logical_and(i >= 5, i < NY + 5))
        def _():
            y_stage2(i - 5)

        @pl.when(i >= 7)
        def _():
            y_stage3(i - 7)

        @pl.when(i < NC)
        def _():
            have_hidden(2 * i)

            @pl.when(i == 1)
            def _():
                z_stage0(2)

            @pl.when(i >= 2)
            def _():
                y_stage0(i - 2)

        products(1, i == 3)

        @pl.when(i < NC)
        def _():
            have_hidden(2 * i + 1)
            z_stage0(i + 2)

        gates(i - 3, jnp.logical_and(i >= 4, i < NC + 3))

        @pl.when(jnp.logical_and(jnp.logical_and(i >= 3, i != 4), i < NC + 4))
        def _():
            loop(jnp.where(i == 3, 0, jnp.where(i == 5, 2, i - 2)), i - 1, z_stage3)

        @pl.when(jnp.logical_and(i >= 2, i < NC + 1))
        def _():
            loop(jnp.where(i == 2, 2, i + 1), i + 2, z_stage1)

        @pl.when(jnp.logical_and(i != 2, i < NC + 2))
        def _():
            loop(jnp.where(i == 1, 0, jnp.where(i == 3, 2, i)), i + 1, z_stage2)

        @pl.when(i == NC + 2)
        def _():
            loop(0, NU, sent)
            loop(0, NC, lambda k: gh_send(k).wait_send())
            loop(0, 4, sent_x)

    loop(1, NC + 5, body)

    loop(0, NZ, sent_z)
    loop(0, NY, sent_y)


def write_out(gate_v, up_v, weight_v, o_gate, o_up, o_weight, sems):
    copies = []
    for src, dst in ((gate_v, o_gate), (up_v, o_up), (weight_v, o_weight)):
        rows = src.shape[0] // 4
        for part in range(4):
            r = pl.ds(part * rows, rows)
            copies.append(pltpu.make_async_copy(src.at[r], dst.at[r], sems.at[len(copies)]))
    for copy in copies:
        copy.start()
    for copy in copies:
        copy.wait()


def on_device(grad_out, gate_pre, up_pre, down_weight):
    dma = pltpu.SemaphoreType.DMA
    vmem = lambda *shape: pltpu.VMEM(shape, BF16)
    scratch = [
        vmem(TOK, DM), vmem(TOK, 8 * BLK), vmem(8 * BLK, 2 * TOK), vmem(2 * TOK, FF),
        vmem(2, FC, DM), vmem(NC, TOK, FC), vmem(NC, HALF, FC),
        vmem(NZ, 2, 2 * BLK, BLK), vmem(NZ, 2, 2 * BLK, BLK), vmem(NZ, 2, 2 * BLK, HF), vmem(NZ, 2, 2 * BLK, HF),
        vmem(NZ, BLK, HF), vmem(NZ, BLK, HF), pltpu.VMEM((NZ, BLK, HF), F32),
        vmem(NY, 4 * BLK, HF), vmem(NY, 4 * BLK, HF), vmem(NY, 2, BLK, BLK), vmem(NY, 2, BLK, BLK),
        vmem(NY, 2, BLK, HF), vmem(NY, 2, BLK, HF), pltpu.VMEM((NY, 3 * BLK, HF), F32),
        dma((16, 2)), dma((16, 2)), dma((16, 2)), dma((16, 2)), dma((8,)), dma((8,)),
        dma((4, 2)), dma((4, 2)), dma((4, 2)), dma((4, 2)),
        dma((NU,)), dma((NU,)), dma((NU,)), dma((NU,)), dma((NU,)), dma((NU,)),
        dma((NZ, 2)), dma((NZ, 2)), dma((NZ, 2)), dma((NZ, 2)), dma((NZ,)), dma((NZ,)),
        dma((NY,)), dma((NY,)), dma((NY, 2)), dma((NY, 2)), dma((NY, 2)), dma((NY, 2)),
        dma((NC,)), dma((NC,)), dma((NC,)), dma((NC,)), dma, dma((2,)),
    ]
    anywhere = pl.BlockSpec(memory_space=pl.ANY)
    results = pl.pallas_call(
        kernel,
        out_shape=(pltpu.VMEM((HALF, FF), BF16), pltpu.VMEM((HALF, FF), BF16), pltpu.VMEM((FF, BLK), BF16)),
        in_specs=[pl.BlockSpec(memory_space=pltpu.HBM)] + [anywhere] * 3,
        out_specs=(pl.BlockSpec(memory_space=pltpu.VMEM),) * 3,
        scratch_shapes=scratch,
        compiler_params=pltpu.CompilerParams(
            collective_id=0, has_side_effects=True, vmem_limit_bytes=48 * 2**20
        ),
        cost_estimate=pl.CostEstimate(flops=4 * TOK * FF * DM, bytes_accessed=24 * 10**6, transcendentals=2 * HALF * FF),
    )(pltpu.with_memory_space_constraint(grad_out[0], pltpu.HBM), gate_pre[0], up_pre[0], down_weight)
    grad_gate, grad_up, grad_weight = pl.pallas_call(
        write_out,
        out_shape=tuple(jax.ShapeDtypeStruct(r.shape, r.dtype) for r in results),
        in_specs=[pl.BlockSpec(memory_space=pltpu.VMEM)] * 3,
        out_specs=(anywhere,) * 3,
        scratch_shapes=[dma((12,))],
        compiler_params=pltpu.CompilerParams(vmem_limit_bytes=2**20),
    )(*(pltpu.with_memory_space_constraint(r, pltpu.VMEM) for r in results))
    return grad_gate[None], grad_up[None], grad_weight


def solution(mesh):
    in_specs = (
        P("depth", "row", "col"),
        P("depth", "col", "row"),
        P("depth", "col", "row"),
        P("row", "col"),
    )
    out_specs = (P("depth", "col", "row"), P("depth", "col", "row"), P("row", ("col", "depth")))
    return jax.shard_map(
        on_device, mesh=mesh, in_specs=in_specs, out_specs=out_specs, check_vma=False
    )
```

```python
import jax
import jax.numpy as jnp
from jax import lax
from jax.experimental import pallas as pl
from jax.experimental.pallas import tpu as pltpu
from jax.sharding import PartitionSpec as P

MESH = pl.DeviceIdType.MESH
BF16, F32 = jnp.bfloat16, jnp.float32

TOK, FF, DM = 512, 3584, 2048
HALF = TOK // 2
ROWS = TOK // 4
FC = 512
NC = FF // FC
HF = FC // 2
NU = FF // HF
NY = 5
NZ = NU - NY
BLK = 128
STEP = 32
SCALE = float(16 * TOK) ** -0.5


def sigmoid(v):
    return 0.5 * jnp.tanh(0.5 * v) + 0.5


def kernel(
    go, gate, up, w, gate_v, up_v, wout,
    g_own, g_pair, g_t, hid, wbuf, ghs, ghr,
    zs0, zr0, zs1, zr1, es, er, zkeep,
    as_, ar, ys0, yr0, ys1, yr1, ykeep,
    xo_s, xo_r, xf_s, xf_r, pp_s, pp_r, px_s, px_r, pf_s, pf_r,
    hc_s, hc_r, hp_s, hp_r, hf_s, hf_r,
    z0_s, z0_r, z1_s, z1_r, e_s, e_r, a_s, a_r, y0_s, y0_r, y1_s, y1_r,
    gh_s, gh_r, ld_g, ld_u, ld_o, ld_w,
):
    x, c, q = lax.axis_index("row"), lax.axis_index("col"), lax.axis_index("depth")
    z, y = lax.div(q, 4), lax.rem(q, 4)
    odd = lax.rem(y, 2)
    y_pair = y + 1 - 2 * odd
    y_sum = lax.rem(y + 3 + 2 * odd, 4)
    y_pair_sum = lax.rem(y_pair + 3 + 2 * (1 - odd), 4)
    core = (x, 1 - c, q)
    right, left = (lax.rem(x + 1, 4), c, q), (lax.rem(x + 3, 4), c, q)
    sides = (right, left)
    pair = (x, c, z * 4 + y_pair)
    across = (x, c, z * 4 + y_sum)
    above, below = (x, c, lax.rem(z + 1, 4) * 4 + y), (x, c, lax.rem(z + 3, 4) * 4 + y)

    barrier = pltpu.get_barrier_semaphore()
    for other in (core, right, left, pair, across, above, below):
        pl.semaphore_signal(barrier, inc=1, device_id=other, device_id_type=MESH)
    def send(src, dst, ss, rs, device):
        return pltpu.make_async_remote_copy(
            src_ref=src, dst_ref=dst, send_sem=ss, recv_sem=rs, device_id=device, device_id_type=MESH
        )

    def ds(start, size, unit):
        return pl.ds(pl.multiple_of(start, unit), size)

    def layer(j):
        return lax.rem(z + jnp.where(j == 0, 2, jnp.where(j == 1, 1, jnp.where(j == 2, 3, 0))), 4)

    def block_of(j, s):
        column = (y, y_sum, y_pair, y_pair_sum)[s]
        return layer(j) * 4 + column

    def cols(b):
        return ds(b * BLK, BLK, BLK)

    def own_copy():
        return pltpu.make_async_copy(go, g_own.at[ds(x * ROWS, ROWS, ROWS)], ld_o)

    def own_direct(b, side):
        return send(
            g_own.at[ds(x * ROWS, ROWS, ROWS), cols(b)], g_own.at[ds(x * ROWS, ROWS, ROWS), cols(b)],
            xo_s.at[b, side], xo_r.at[b, side], sides[side],
        )

    def own_forward(b, side):
        source = lax.rem(x + (3 if side == 0 else 1), 4)
        rows = ds(source * ROWS + side * (ROWS // 2), ROWS // 2, ROWS // 2)
        return send(
            g_own.at[rows, cols(b)], g_own.at[rows, cols(b)], xf_s.at[b, side], xf_r.at[b, side], sides[side]
        )

    def pair_send(j, s):
        i = j * 2 + s
        return send(
            g_own.at[ds(x * ROWS, ROWS, ROWS), cols(block_of(j, s + 2))], g_pair.at[ds(x * ROWS, ROWS, ROWS), cols(i)],
            pp_s.at[i], pp_r.at[i], pair,
        )

    def pair_cols(j):
        return ds(j * 2 * BLK, 2 * BLK, 2 * BLK)

    def pair_direct(j, side):
        view = g_pair.at[ds(x * ROWS, ROWS, ROWS), pair_cols(j)]
        return send(view, view, px_s.at[j, side], px_r.at[j, side], sides[side])

    def pair_forward(j, side):
        source = lax.rem(x + (3 if side == 0 else 1), 4)
        view = g_pair.at[ds(source * ROWS + side * (ROWS // 2), ROWS // 2, ROWS // 2), pair_cols(j)]
        return send(view, view, pf_s.at[j, side], pf_r.at[j, side], sides[side])

    def own_start(j, first):
        for s in (first, first + 1):
            for side in (0, 1):
                own_direct(block_of(j, s), side).start()

    def own_pass(j, first):
        for s in (first, first + 1):
            b = block_of(j, s)
            for side in (0, 1):
                own_direct(b, side).wait_recv()
                own_forward(b, side).start()

    def own_end(j, first):
        for s in (first, first + 1):
            for side in (0, 1):
                own_forward(block_of(j, s), side).wait_recv()

    def in_copy(k, src, dst, sem):
        f = ds(k * FC, FC, FC)
        return pltpu.make_async_copy(src.at[:, f], dst.at[:, f], sem.at[k])

    def hid_view(group, u):
        return hid.at[ds(group * TOK + c * HALF, HALF, HALF), ds(u * HF, HF, HF)]

    def hid_core(u):
        return send(hid_view(0, u), hid_view(0, u), hc_s.at[u], hc_r.at[u], core)

    def hid_pair(u):
        return send(hid_view(0, u), hid_view(1, u), hp_s.at[u], hp_r.at[u], pair)

    def hid_pass(u):
        return send(hid_view(1, u), hid_view(1, u), hf_s.at[u], hf_r.at[u], core)

    def pass_on(u):
        hid_pair(u).wait_recv()
        hid_pass(u).start()

    def have_hidden(u):
        hid_core(u).wait_recv()
        hid_pass(u).wait_recv()

    def make_hidden(k):
        in_copy(k, gate, gate_v, ld_g).wait()
        in_copy(k, up, up_v, ld_u).wait()
        f = ds(k * FC, FC, FC)

        def rows(i, carry):
            r = ds(i * STEP, STEP, STEP)
            g = gate_v[r, f].astype(F32)
            u = up_v[r, f].astype(F32)
            hid[ds(c * HALF + i * STEP, STEP, STEP), f] = (g * sigmoid(g) * u).astype(BF16)
            return carry

        lax.fori_loop(0, HALF // STEP, rows, 0)
        for u in (2 * k, 2 * k + 1):
            hid_pair(u).start()
            hid_core(u).start()

    def dot(rows, u):
        return jnp.dot(rows, hid[:, ds(u * HF, HF, HF)], preferred_element_type=F32)

    def unit_z(k):
        return jnp.maximum(k, 2 * k - 3)

    def unit_y(k):
        return 2 * k + 4

    def of_layer(j):
        return g_t[2 * BLK * j : 2 * BLK * (j + 1), :]

    def of_column(s, h):
        return jnp.concatenate(
            [g_t[(4 * h + s) * BLK : (4 * h + s + 1) * BLK, :], g_t[(4 * h + 2 + s) * BLK : (4 * h + 3 + s) * BLK, :]], 0
        )

    def z0(k, half):
        return send(zs0.at[k, half], zr0.at[k, half], z0_s.at[k, half], z0_r.at[k, half], (below, above)[half])

    def z1(k, way):
        return send(zs1.at[k, way], zr1.at[k, way], z1_s.at[k, way], z1_r.at[k, way], (above, below)[way])

    def z_last(k):
        return send(es.at[k], er.at[k], e_s.at[k], e_r.at[k], across)

    def y_first(k):
        return send(as_.at[k], ar.at[k], a_s.at[k], a_r.at[k], across)

    def y0(k, half):
        return send(ys0.at[k, half], yr0.at[k, half], y0_s.at[k, half], y0_r.at[k, half], (below, above)[half])

    def y1(k, way):
        return send(ys1.at[k, way], yr1.at[k, way], y1_s.at[k, way], y1_r.at[k, way], (above, below)[way])

    def z_stage0(k):
        part = dot(of_layer(0), unit_z(k)).astype(BF16)
        for half in (0, 1):
            zs0[k, half] = part[:, half * BLK : (half + 1) * BLK]
            z0(k, half).start()

    def y_stage0(k):
        for h in (0, 1):
            as_[k, 2 * BLK * h : 2 * BLK * (h + 1), :] = dot(of_column(1, h), unit_y(k)).astype(BF16)
        y_first(k).start()

    def z_stage1(k):
        for way in (0, 1):
            part = dot(of_layer(1 + way), unit_z(k))
            half = 1 - way
            z0(k, half).wait_recv()
            lo, hi = part[:, :BLK], part[:, BLK:]
            got = zr0[k, half].astype(F32)
            if half:
                hi = hi + got
            else:
                lo = lo + got
            zs1[k, way, :, :BLK] = lo.astype(BF16)
            zs1[k, way, :, BLK:] = hi.astype(BF16)
            z1(k, way).start()

    def y_stage1(k):
        parts = [dot(of_column(0, h), unit_y(k)) for h in (0, 1)]
        y_first(k).wait_recv()
        first = parts[0] + ar[k, : 2 * BLK, :].astype(F32)
        far = first[:BLK, :].astype(BF16)
        for half in (0, 1):
            ys0[k, half] = far[:, half * BLK : (half + 1) * BLK]
            y0(k, half).start()
        ykeep[k, :BLK, :] = first[BLK:, :]
        ykeep[k, BLK:, :] = parts[1] + ar[k, 2 * BLK :, :].astype(F32)

    def z_stage2(k):
        part = dot(of_layer(3), unit_z(k))
        for way in (0, 1):
            z1(k, way).wait_recv()
            part = part + zr1[k, way].astype(F32)
        es[k] = part[BLK:, :].astype(BF16)
        z_last(k).start()
        zkeep[k] = part[:BLK, :]

    def y_stage2(k):
        for way in (0, 1):
            half = 1 - way
            y0(k, half).wait_recv()
            got = yr0[k, half].astype(F32)
            lo, hi = ykeep[k, BLK * way : BLK * (way + 1), :BLK], ykeep[k, BLK * way : BLK * (way + 1), BLK:]
            if half:
                hi = hi + got
            else:
                lo = lo + got
            ys1[k, way, :, :BLK] = lo.astype(BF16)
            ys1[k, way, :, BLK:] = hi.astype(BF16)
            y1(k, way).start()

    def z_stage3(k):
        z_last(k).wait_recv()
        total = zkeep[k] + er[k].astype(F32)
        wout[ds(unit_z(k) * HF, HF, HF), :] = (total * SCALE).T.astype(BF16)

    def y_stage3(k):
        total = ykeep[k, 2 * BLK :, :]
        for way in (0, 1):
            y1(k, way).wait_recv()
            total = total + yr1[k, way].astype(F32)
        wout[ds(unit_y(k) * HF, HF, HF), :] = (total * SCALE).T.astype(BF16)

    def w_copy(k):
        slot = lax.rem(k, 2)
        return pltpu.make_async_copy(w.at[ds(k * FC, FC, FC)], wbuf.at[slot], ld_w.at[slot])

    def gh_send(k):
        return send(ghs.at[k, ds((1 - c) * HALF, HALF, HALF)], ghr.at[k], gh_s.at[k], gh_r.at[k], core)

    def grad_hidden(k):
        w_copy(k).wait()

        def tile(n, carry):
            f = ds(n * HF, HF, HF)
            ghs[k, :, f] = lax.dot_general(
                g_own[...], wbuf[lax.rem(k, 2), f, :], (((1,), (1,)), ((), ())), preferred_element_type=F32
            ).astype(BF16)
            return carry

        lax.fori_loop(0, 2, tile, 0)
        gh_send(k).start()

        @pl.when(k + 2 < NC)
        def _():
            w_copy(k + 2).start()

    def grad_gate(k):
        gh_send(k).wait_recv()
        f = ds(k * FC, FC, FC)

        def rows(i, carry):
            r = ds(i * STEP, STEP, STEP)
            g = gate_v[r, f].astype(F32)
            u = up_v[r, f].astype(F32)
            grad = ghs[k, ds(c * HALF + i * STEP, STEP, STEP), :].astype(F32) + ghr[k, r, :].astype(F32)
            sig = sigmoid(g)
            gate_v[r, f] = (grad * u * (sig * (1.0 + g * (1.0 - sig)))).astype(BF16)
            up_v[r, f] = (grad * (g * sig)).astype(BF16)
            return carry

        lax.fori_loop(0, HALF // STEP, rows, 0)

    def sent(u):
        hid_core(u).wait_send()
        hid_pair(u).wait_send()
        hid_pass(u).wait_send()

    def sent_z(k):
        for i in (0, 1):
            z0(k, i).wait_send()
            z1(k, i).wait_send()
        z_last(k).wait_send()

    def sent_y(k):
        for i in (0, 1):
            y0(k, i).wait_send()
            y1(k, i).wait_send()
        y_first(k).wait_send()

    def sent_x(j):
        for s in range(4):
            for side in (0, 1):
                own_direct(block_of(j, s), side).wait_send()
                own_forward(block_of(j, s), side).wait_send()
        for s in (0, 1):
            pair_send(j, s).wait_send()
        for side in (0, 1):
            pair_direct(j, side).wait_send()
            pair_forward(j, side).wait_send()

    def loop(lo, hi, step):
        def run(i, carry):
            step(i)
            return carry

        lax.fori_loop(lo, hi, run, 0)

    def load(k):
        in_copy(k, gate, gate_v, ld_g).start()
        in_copy(k, up, up_v, ld_u).start()

    def pair_start(j):
        for s in (0, 1):
            pair_send(j, s).start()

    own_copy().start()
    loop(0, NC, load)
    w_copy(0).start()
    w_copy(1).start()
    own_copy().wait()
    pl.semaphore_wait(barrier, 7)
    own_start(0, 0)
    pair_start(0)
    own_start(1, 0)
    pair_start(1)

    make_hidden(0)
    pair_start(2)
    pair_start(3)
    loop(1, 5, make_hidden)

    def turn(j):
        own_end(j, 0)
        for side in (0, 1):
            pair_forward(j, side).wait_recv()
        for s in (0, 1):
            rows = ds((j * 2 + s) * BLK, BLK, BLK)
            g_t[rows, :TOK] = g_own[:, cols(block_of(j, s))].T
            g_t[rows, TOK:] = g_pair[:, cols(j * 2 + s)].T

    def gather(t):
        @pl.when(jnp.logical_and(t >= 2, t < 4))
        def _():
            pass_on(t - 2)

        @pl.when(t >= 2)
        def _():
            turn(t - 2)

        @pl.when(t == 4)
        def _():
            loop(0, 2, z_stage1)

        @pl.when(jnp.logical_and(t >= 1, t < 5))
        def _():
            for side in (0, 1):
                pair_direct(t - 1, side).wait_recv()
                pair_forward(t - 1, side).start()

        @pl.when(t == 4)
        def _():
            loop(0, 4, lambda j: own_start(j, 2))

        @pl.when(t < 4)
        def _():
            for s in (0, 1):
                pair_send(t, s).wait_recv()
            for side in (0, 1):
                pair_direct(t, side).start()

        @pl.when(t < 2)
        def _():
            own_start(t + 2, 0)

        @pl.when(t < 4)
        def _():
            own_pass(t, 0)

        @pl.when(jnp.logical_and(t >= 2, t < 4))
        def _():
            have_hidden(t - 2)
            z_stage0(t - 2)

        @pl.when(t + 5 < NC)
        def _():
            make_hidden(t + 5)

    loop(0, 6, gather)

    def products(k, on):
        @pl.when(on)
        def _():
            grad_hidden(k)

    def gates(k, on):
        @pl.when(on)
        def _():
            grad_gate(k)

    def body(i):
        @pl.when(i < NC)
        def _():
            pass_on(2 * i)

        @pl.when(i == 2)
        def _():
            loop(0, 4, lambda j: own_pass(j, 2))

        @pl.when(i == 3)
        def _():
            loop(0, 4, lambda j: own_end(j, 2))

        products(jnp.where(i == 3, 0, i - 2), jnp.logical_and(i >= 3, i < NC + 2))

        @pl.when(i < NC)
        def _():
            pass_on(2 * i + 1)

        gates(0, i == 4)

        @pl.when(jnp.logical_and(i >= 4, i < NY + 4))
        def _():
            y_stage1(i - 4)

        @pl.when(jnp.logical_and(i >= 5, i < NY + 5))
        def _():
            y_stage2(i - 5)

        @pl.when(i >= 7)
        def _():
            y_stage3(i - 7)

        @pl.when(i < NC)
        def _():
            have_hidden(2 * i)

            @pl.when(i == 1)
            def _():
                z_stage0(2)

            @pl.when(i >= 2)
            def _():
                y_stage0(i - 2)

        products(1, i == 3)

        @pl.when(i < NC)
        def _():
            have_hidden(2 * i + 1)
            z_stage0(i + 2)

        gates(i - 3, jnp.logical_and(i >= 4, i < NC + 3))

        @pl.when(jnp.logical_and(jnp.logical_and(i >= 3, i != 4), i < NC + 4))
        def _():
            loop(jnp.where(i == 3, 0, jnp.where(i == 5, 2, i - 2)), i - 1, z_stage3)

        @pl.when(jnp.logical_and(i >= 2, i < NC + 1))
        def _():
            loop(jnp.where(i == 2, 2, i + 1), i + 2, z_stage1)

        @pl.when(jnp.logical_and(i != 2, i < NC + 2))
        def _():
            loop(jnp.where(i == 1, 0, jnp.where(i == 3, 2, i)), i + 1, z_stage2)

        @pl.when(i == NC + 2)
        def _():
            loop(0, NU, sent)
            loop(0, NC, lambda k: gh_send(k).wait_send())
            loop(0, 4, sent_x)

    loop(1, NC + 5, body)

    loop(0, NZ, sent_z)
    loop(0, NY, sent_y)


def write_out(gate_v, up_v, weight_v, o_gate, o_up, o_weight, sems):
    copies = []
    for src, dst in ((gate_v, o_gate), (up_v, o_up), (weight_v, o_weight)):
        rows = src.shape[0] // 4
        for part in range(4):
            r = pl.ds(part * rows, rows)
            copies.append(pltpu.make_async_copy(src.at[r], dst.at[r], sems.at[len(copies)]))
    for copy in copies:
        copy.start()
    for copy in copies:
        copy.wait()


def on_device(grad_out, gate_pre, up_pre, down_weight):
    dma = pltpu.SemaphoreType.DMA
    vmem = lambda *shape: pltpu.VMEM(shape, BF16)
    scratch = [
        vmem(TOK, DM), vmem(TOK, 8 * BLK), vmem(8 * BLK, 2 * TOK), vmem(2 * TOK, FF),
        vmem(2, FC, DM), vmem(NC, TOK, FC), vmem(NC, HALF, FC),
        vmem(NZ, 2, 2 * BLK, BLK), vmem(NZ, 2, 2 * BLK, BLK), vmem(NZ, 2, 2 * BLK, HF), vmem(NZ, 2, 2 * BLK, HF),
        vmem(NZ, BLK, HF), vmem(NZ, BLK, HF), pltpu.VMEM((NZ, BLK, HF), F32),
        vmem(NY, 4 * BLK, HF), vmem(NY, 4 * BLK, HF), vmem(NY, 2, BLK, BLK), vmem(NY, 2, BLK, BLK),
        vmem(NY, 2, BLK, HF), vmem(NY, 2, BLK, HF), pltpu.VMEM((NY, 3 * BLK, HF), F32),
        dma((16, 2)), dma((16, 2)), dma((16, 2)), dma((16, 2)), dma((8,)), dma((8,)),
        dma((4, 2)), dma((4, 2)), dma((4, 2)), dma((4, 2)),
        dma((NU,)), dma((NU,)), dma((NU,)), dma((NU,)), dma((NU,)), dma((NU,)),
        dma((NZ, 2)), dma((NZ, 2)), dma((NZ, 2)), dma((NZ, 2)), dma((NZ,)), dma((NZ,)),
        dma((NY,)), dma((NY,)), dma((NY, 2)), dma((NY, 2)), dma((NY, 2)), dma((NY, 2)),
        dma((NC,)), dma((NC,)), dma((NC,)), dma((NC,)), dma, dma((2,)),
    ]
    anywhere = pl.BlockSpec(memory_space=pl.ANY)
    results = pl.pallas_call(
        kernel,
        out_shape=(pltpu.VMEM((HALF, FF), BF16), pltpu.VMEM((HALF, FF), BF16), pltpu.VMEM((FF, BLK), BF16)),
        in_specs=[pl.BlockSpec(memory_space=pltpu.HBM)] + [anywhere] * 3,
        out_specs=(pl.BlockSpec(memory_space=pltpu.VMEM),) * 3,
        scratch_shapes=scratch,
        compiler_params=pltpu.CompilerParams(
            collective_id=0, has_side_effects=True, vmem_limit_bytes=48 * 2**20
        ),
        cost_estimate=pl.CostEstimate(flops=4 * TOK * FF * DM, bytes_accessed=24 * 10**6, transcendentals=2 * HALF * FF),
    )(pltpu.with_memory_space_constraint(grad_out[0], pltpu.HBM), gate_pre[0], up_pre[0], down_weight)
    grad_gate, grad_up, grad_weight = pl.pallas_call(
        write_out,
        out_shape=tuple(jax.ShapeDtypeStruct(r.shape, r.dtype) for r in results),
        in_specs=[pl.BlockSpec(memory_space=pltpu.VMEM)] * 3,
        out_specs=(anywhere,) * 3,
        scratch_shapes=[dma((12,))],
        compiler_params=pltpu.CompilerParams(vmem_limit_bytes=2**20),
    )(*(pltpu.with_memory_space_constraint(r, pltpu.VMEM) for r in results))
    return grad_gate[None], grad_up[None], grad_weight


def solution(mesh):
    in_specs = (
        P("depth", "row", "col"),
        P("depth", "col", "row"),
        P("depth", "col", "row"),
        P("row", "col"),
    )
    out_specs = (P("depth", "col", "row"), P("depth", "col", "row"), P("row", ("col", "depth")))
    return jax.shard_map(
        on_device, mesh=mesh, in_specs=in_specs, out_specs=out_specs, check_vma=False
    )
```
